32 devices in a mesh: dp: 4 (over y, x), lon: 8 (over z, core).
Axes of the slice: x: 2, y: 2, z: 4, core: 2. Of those that a mesh axis runs over, the one named last changes fastest.
Arguments:
- fields: bfloat16 [4, 64, 128, 384], P('dp', None, 'lon'), may hold values from -6 to 6
- cotangent: bfloat16 [4, 64, 128, 384], P('dp', None, 'lon'), may hold values from -6 to 6
- kernel_first: bfloat16 [3, 3, 64, 64], replicated, may hold values from -0.25 to 0.25
- kernel_second: bfloat16 [3, 3, 64, 64], replicated, may hold values from -0.25 to 0.25
- metric: float32 [384], replicated, may hold values from 0.5 to 3
Outputs:
- field_grad: bfloat16 [4, 64, 128, 384], P('dp', None, 'lon')
- grad_first: bfloat16 [3, 3, 64, 64], replicated
- grad_second: bfloat16 [3, 3, 64, 64], replicated
The draws below stay inside these ranges and needn't reach their ends.
All inputs are finite; a program needn't handle non-finite values.
Results may differ from the reference program's by a relative error of at most 0.0063.
Values may be sent and summed in bfloat16 or wider, within the bound.
No kernel may reach another device: no remote copies, remote signals or barrier semaphores. Data moves between devices by JAX's collectives and lax.ppermute only.
A program may use at most 64 MiB of HBM per device.

```python
import math
import jax
import jax.numpy as jnp
from jax import lax

C = 64
LAT = 384
LON = 128
SAMPLES = 4


def levels(own_key, dims, cuts, least, largest):
    loudness = 1.0
    for position, blocks in cuts:
        draws = jax.random.uniform(jax.random.fold_in(jax.random.fold_in(own_key, 6), position), (blocks,), jnp.float32, least / len(cuts), largest / len(cuts))
        loudness = loudness * jnp.repeat(jnp.exp(draws), dims[position] // blocks).reshape((-1,) + (1,) * (len(dims) - 1 - position))
    return loudness


def scatter_about(key, shape, deviation, most, split=(), kind=jnp.bfloat16):
    loudness = levels(key, shape, split, -0.22, 0.18) if split else 1.0
    array = jax.random.normal(key, shape, jnp.float32) * deviation * loudness
    return jnp.minimum(jnp.maximum(array, -most), most).astype(kind)


def setup_inputs(seed: int = 0) -> dict:
    key_list = jax.random.split(jax.random.key(seed), 6)
    fields = scatter_about(key_list[0], (SAMPLES, C, LON, LAT), 1.0, 6.0, ((0, 4), (2, 8)))
    cotangent = scatter_about(key_list[1], (SAMPLES, C, LON, LAT), 1.0, 6.0, ((0, 4), (2, 8)))
    kernel_first = scatter_about(key_list[2], (3, 3, C, C), (9 * C) ** -0.5, 0.25)
    kernel_second = scatter_about(key_list[3], (3, 3, C, C), (9 * C) ** -0.5, 0.25)
    metric = jnp.clip(jnp.exp(jax.random.uniform(key_list[4], (LAT,), jnp.float32, math.log(0.5), math.log(3.0))), 0.5, 3.0)
    return {"fields": fields, "cotangent": cotangent, "kernel_first": kernel_first, "kernel_second": kernel_second, "metric": metric}


gelu_coef = 0.7978845608


def gelu_value(u):
    inner = jnp.tanh(gelu_coef * (u + 0.044715 * u * u * u))
    return 0.5 * u * (1.0 + inner)


def gelu_slope(u):
    inner = jnp.tanh(gelu_coef * (u + 0.044715 * u * u * u))
    return 0.5 * (1.0 + inner) + 0.5 * u * (1.0 - inner * inner) * gelu_coef * (1.0 + 3.0 * 0.044715 * u * u)


def pad_rows(value):
    return jnp.pad(value, ((0, 0), (0, 0), (1, 1)))


def stencil_apply(value, taps, metric):
    padded = pad_rows(value).astype(jnp.float32)
    total = jnp.zeros((taps.shape[2], value.shape[1], LAT), jnp.float32)
    for p in range(3):
        moved = jnp.roll(padded, -(p - 1), axis=1)
        summed = jnp.zeros_like(total)
        for q in range(3):
            summed = summed + jnp.einsum("oc,cij->oij", taps[p, q].astype(jnp.float32), moved[:, :, q:q + LAT])
        total = total + (summed if p == 1 else summed * metric[None, None, :])
    return total


def stencil_adjoint(plain, scaled, taps):
    total = jnp.zeros((taps.shape[3], plain.shape[1], LAT), jnp.float32)
    for p in range(3):
        source = pad_rows(plain if p == 1 else scaled).astype(jnp.float32)
        moved = jnp.roll(source, p - 1, axis=1)
        for q in range(3):
            total = total + jnp.einsum("oc,oij->cij", taps[p, q].astype(jnp.float32), moved[:, :, 2 - q:2 - q + LAT])
    return total


def kernel_term(plain, scaled, value):
    padded = pad_rows(value).astype(jnp.float32)
    terms = []
    for p in range(3):
        source = (plain if p == 1 else scaled).astype(jnp.float32)
        moved = jnp.roll(padded, -(p - 1), axis=1)
        row_terms = []
        for q in range(3):
            row_terms.append(jnp.einsum("oij,cij->oc", source, moved[:, :, q:q + LAT]))
        terms.append(jnp.stack(row_terms))
    return jnp.stack(terms)


def reference(fields, cotangent, kernel_first, kernel_second, metric):
    scale_row = metric[None, None, :]

    def one_sample(carry, pair):
        sample, upstream = pair
        before_gelu = stencil_apply(sample, kernel_first, metric)
        hidden = gelu_value(before_gelu).astype(jnp.bfloat16)
        upstream_scaled = (scale_row * upstream.astype(jnp.float32)).astype(jnp.bfloat16)
        second = kernel_term(upstream, upstream_scaled, hidden)
        hidden_grad = stencil_adjoint(upstream, upstream_scaled, kernel_second)
        delta = (hidden_grad * gelu_slope(before_gelu)).astype(jnp.bfloat16)
        delta_scaled = (scale_row * delta.astype(jnp.float32)).astype(jnp.bfloat16)
        first = kernel_term(delta, delta_scaled, sample)
        result = (upstream.astype(jnp.float32) + stencil_adjoint(delta, delta_scaled, kernel_first)).astype(jnp.bfloat16)
        return (carry[0] + first, carry[1] + second), result

    start = (jnp.zeros((3, 3, C, C), jnp.float32), jnp.zeros((3, 3, C, C), jnp.float32))
    sums, field_grad = lax.scan(one_sample, start, (fields, cotangent))
    factor = jnp.float32(1.0 / (float(SAMPLES) * float(LON) * float(LAT)) ** 0.5)
    return field_grad, (sums[0] * factor).astype(jnp.bfloat16), (sums[1] * factor).astype(jnp.bfloat16)
```

```python
import functools

import jax
import jax.numpy as jnp
from jax import lax
from jax.experimental import pallas as pl
from jax.experimental.pallas import tpu as pltpu
from jax.sharding import PartitionSpec as P

gelu_coef = 0.7978845608
F32 = jnp.float32
BF16 = jnp.bfloat16
NT = (((1,), (1,)), ((), ()))


def gelu_pair(u):
    inner = jnp.tanh(gelu_coef * (u + 0.044715 * u * u * u))
    value = 0.5 * u * (1.0 + inner)
    slope = 0.5 * (1.0 + inner) + 0.5 * u * (1.0 - inner * inner) * gelu_coef * (
        1.0 + 3.0 * 0.044715 * u * u
    )
    return value, slope


def neighbours(v):
    lat = v.shape[-1]
    row = lax.broadcasted_iota(jnp.int32, v.shape, 1)
    zero = jnp.zeros_like(v)
    below = jnp.where(row == 0, zero, pltpu.roll(v, 1, 1))
    above = jnp.where(row == lat - 1, zero, pltpu.roll(v, lat - 1, 1))
    return below, above


def dot(a, b):
    return jnp.dot(a, b, preferred_element_type=F32)


def dot_nt(a, b):
    return lax.dot_general(a, b, NT, preferred_element_type=F32)


def put_three(ref, index, v, adjoint):
    channels = v.shape[0]
    below, above = neighbours(v)
    if adjoint:
        below, above = above, below
    ref[index, 0:channels, :] = below.astype(BF16)
    ref[index, channels : 2 * channels, :] = v.astype(BF16)
    ref[index, 2 * channels :, :] = above.astype(BF16)


def prepare(k_ref, forward_ref, adjoint_ref):
    c = k_ref.shape[-1]
    for p in range(3):
        if forward_ref is not None:
            forward_ref[p * c : (p + 1) * c, :] = jnp.concatenate(
                [k_ref[p, q].astype(F32) for q in range(3)], axis=1
            ).astype(BF16)
        adjoint_ref[p * c : (p + 1) * c, :] = jnp.concatenate(
            [k_ref[p, q].astype(F32).T for q in range(3)], axis=1
        ).astype(BF16)


def spread(i, x, e, metric, x3, e3, s3):
    put_three(x3, i, x, False)
    put_three(e3, i, e, True)
    scaled = (metric * e).astype(BF16).astype(F32)
    put_three(s3, i, scaled, True)


def products(i, w1, w2a, x3, e3, s3, y, z):
    c = x3.shape[1] // 3
    y[i] = dot(w1[...], x3[i])
    z[i, c : 2 * c, :] = dot(w2a[c : 2 * c, :], e3[i])
    sides = dot(jnp.concatenate([w2a[0:c, :], w2a[2 * c :, :]], axis=0), s3[i])
    z[i, 0:c, :] = sides[0:c]
    z[i, 2 * c :, :] = sides[c:]


def middle(i, metric, y, z):
    c = y.shape[1] // 3
    u = y[i, c : 2 * c, :] + metric * (y[i - 1, 0:c, :] + y[i + 1, 2 * c :, :])
    hidden, slope = gelu_pair(u)
    grad = z[i, c : 2 * c, :] + (z[i + 1, 0:c, :] + z[i - 1, 2 * c :, :])
    delta = (grad * slope).astype(BF16).astype(F32)
    return hidden.astype(BF16).astype(F32), delta, (metric * delta).astype(BF16).astype(F32)


def three_rows(plain, scaled, j):
    c = plain.shape[1] // 3
    mid = slice(c, 2 * c)
    return jnp.concatenate(
        [scaled[j + 1, mid, :], plain[j, mid, :], scaled[j - 1, mid, :]], axis=0
    )


def scatter_out(ref, value):
    c, n, lat = value.shape
    value = value.astype(F32).reshape(c * n, lat)
    for k in range(lat // 128):
        ref[k * c * n : (k + 1) * c * n, :] = value[:, k * 128 : (k + 1) * 128]


def strided(ref, i, c, n):
    count = ref.shape[0] // (c * n)
    return [(k, pl.ds(k * c * n + i, c, stride=n)) for k in range(count)]


def column(ref, i, c, n):
    return jnp.concatenate([ref[at, :] for _, at in strided(ref, i, c, n)], axis=1)


def interior_kernel(
    x_ref, e_ref, k1_ref, k2_ref, m_ref,
    g1_ref, g2_ref, d_ref, s_ref, w1_ref, w1a_ref, w2a_ref,
    xf, ef, x3, e3, s3, y, z, h3,
):
    c, n, lat = x_ref.shape
    metric = m_ref[...]
    prepare(k1_ref, w1_ref, w1a_ref)
    prepare(k2_ref, None, w2a_ref)
    scatter_out(xf, x_ref[...])
    scatter_out(ef, e_ref[...])

    def first_pass(i, carry):
        spread(i, column(xf, i, c, n), column(ef, i, c, n), metric, x3, e3, s3)
        products(i, w1_ref, w2a_ref, x3, e3, s3, y, z)
        return carry

    lax.fori_loop(0, n, first_pass, 0, unroll=2)

    blank = jnp.zeros((c, lat), BF16)
    for i in (0, n - 1):
        d_ref[i] = blank
        s_ref[i] = blank

    def second_pass(i, carry):
        hidden, delta, scaled = middle(i, metric, y, z)
        put_three(h3, i, hidden, False)
        d_ref[i] = delta.astype(BF16)
        s_ref[i] = scaled.astype(BF16)
        return carry

    lax.fori_loop(1, n - 1, second_pass, 0, unroll=2)

    g2_ref[...] = jnp.zeros_like(g2_ref)
    g1_ref[...] = jnp.zeros_like(g1_ref)
    for j in (0, n - 1):
        inner = 1 if j == 0 else n - 2
        rows = slice(0, c) if j == 0 else slice(2 * c, 3 * c)
        g1_ref[rows, :] += dot_nt(s_ref[inner], x3[j])

    def third_pass(j, carry):
        g2_ref[...] += dot_nt(three_rows(e3, s3, j), h3[j])
        left = jnp.concatenate([s_ref[j + 1], d_ref[j], s_ref[j - 1]], axis=0)
        g1_ref[...] += dot_nt(left, x3[j])
        return carry

    lax.fori_loop(1, n - 1, third_pass, 0, unroll=2)


def edge_kernel(
    before_ref, first_ref, last_ref, after_ref, m_ref, w1_ref, w2a_ref, g1_in, g2_in,
    g1_ref, g2_ref, d_ref, s_ref,
    x3, e3, s3, y, z, h3,
):
    metric = m_ref[...]
    c = before_ref.shape[2]
    total1, total2 = g1_in[...], g2_in[...]
    for side, pair in ((0, (before_ref, first_ref)), (1, (last_ref, after_ref))):
        base = 4 * side
        for k in range(4):
            source = pair[k // 2]
            spread(
                base + k, source[0, k % 2].astype(F32), source[1, k % 2].astype(F32), metric, x3, e3, s3
            )
            products(base + k, w1_ref, w2a_ref, x3, e3, s3, y, z)
        own = 2 if side == 0 else 1
        for k in (1, 2):
            hidden, delta, scaled = middle(base + k, metric, y, z)
            d_ref[2 * side + k - 1] = delta.astype(BF16)
            s_ref[2 * side + k - 1] = scaled.astype(BF16)
            if k == own:
                put_three(h3, side, hidden, False)
        j = base + own
        total2 = total2 + dot_nt(three_rows(e3, s3, j), h3[side])
        delta, scaled = d_ref[2 * side + own - 1], s_ref[2 * side + own - 1]
        total1 = total1 + jnp.concatenate(
            [dot_nt(scaled, x3[j - 1]), dot_nt(delta, x3[j]), dot_nt(scaled, x3[j + 1])], axis=0
        )
    for ref, total in ((g1_ref, total1), (g2_ref, total2)):
        half = total.shape[0] // 2
        tail = total[:, 2 * c :]
        ref[0 : 2 * half, :] = total[:, 0 : 2 * c].astype(BF16)
        ref[2 * half :, :] = jnp.concatenate([tail[0:half], tail[half:]], axis=1).astype(BF16)


def field_kernel(
    e_ref, d_in, s_in, de_ref, se_ref, w1a_ref, out_ref,
    d3, s3, zm, zs, ef,
):
    c, n, lat = e_ref.shape
    for place, edge in ((0, 0), (1, 1), (n, 2), (n + 1, 3)):
        put_three(d3, place, de_ref[edge].astype(F32), True)
        put_three(s3, place, se_ref[edge].astype(F32), True)

    def fill(i, carry):
        put_three(d3, i + 1, d_in[i].astype(F32), True)
        put_three(s3, i + 1, s_in[i].astype(F32), True)
        return carry

    lax.fori_loop(1, n - 1, fill, 0, unroll=2)

    sides = jnp.concatenate([w1a_ref[0:c, :], w1a_ref[2 * c :, :]], axis=0)

    def multiply(i, carry):
        zm[i] = dot(w1a_ref[c : 2 * c, :], d3[i])
        zs[i] = dot(sides, s3[i])
        return carry

    lax.fori_loop(0, n + 2, multiply, 0, unroll=2)
    scatter_out(ef, e_ref[...])

    def add(i, carry):
        place = i + 1
        grad = zm[place] + (zs[place + 1, 0:c, :] + zs[place - 1, c:, :])
        for k, at in strided(ef, i, c, n):
            ef[at, :] = ef[at, :] + grad[:, k * 128 : (k + 1) * 128]
        return carry

    lax.fori_loop(0, n, add, 0, unroll=2)
    for k in range(lat // 128):
        part = ef[k * c * n : (k + 1) * c * n, :].reshape(c, n, 128)
        out_ref[:, :, k * 128 : (k + 1) * 128] = part.astype(BF16)


def final_kernel(one_ref, two_ref, out1_ref, out2_ref):
    c = out1_ref.shape[-1]
    half = (one_ref.shape[0] // 3)
    for ref, out in ((one_ref, out1_ref), (two_ref, out2_ref)):
        for p in range(3):
            rows = slice(p * c, (p + 1) * c)
            out[p, 0] = ref[rows, 0:c]
            out[p, 1] = ref[rows, c : 2 * c]
        tail = ref[2 * half :, :]
        tail = jnp.concatenate([tail[:, 0:c], tail[:, c:]], axis=0)
        for p in range(3):
            out[p, 2] = tail[p * c : (p + 1) * c]


def vmem(count):
    return [pl.BlockSpec(memory_space=pltpu.VMEM)] * count


def call(kernel, outs, scratch, *args, flops=0):
    return pl.pallas_call(
        kernel,
        out_shape=[jax.ShapeDtypeStruct(s, d) for s, d in outs],
        in_specs=vmem(len(args)),
        out_specs=vmem(len(outs)),
        scratch_shapes=[pltpu.VMEM(s, d) for s, d in scratch],
        compiler_params=pltpu.CompilerParams(vmem_limit_bytes=56 * 2**20),
    )(*args)


def exchange(value, pairs):
    return lax.ppermute(value, ("dp", "lon"), pairs)


def one_sample(x, e, kernel_first, kernel_second, metric):
    c, n, lat = x.shape
    wide = 3 * c
    size = lax.axis_size("lon")
    up = [(i, (i + 1) % size) for i in range(size)]
    down = [(j, i) for i, j in up]
    both = jnp.stack((x, e))
    first = jnp.swapaxes(both[:, :, 0:2], 1, 2)
    last = jnp.swapaxes(both[:, :, n - 2 :], 1, 2)
    before = lax.ppermute(last, "lon", up)
    after = lax.ppermute(first, "lon", down)
    three = (wide, lat)
    g1, g2, d, s, w1, w1a, w2a = call(
        interior_kernel,
        [((wide, wide), F32)] * 2 + [((n, c, lat), BF16)] * 2 + [((wide, wide), BF16)] * 3,
        [((c * n * lat // 128, 128), F32)] * 2
        + [((n,) + three, BF16)] * 3
        + [((n,) + three, F32)] * 2
        + [((n,) + three, BF16)],
        x, e, kernel_first, kernel_second, metric,
    )
    packed = ((3 * wide // 2, 2 * c), BF16)
    p1, p2, de, se = call(
        edge_kernel,
        [packed] * 2 + [((4, c, lat), BF16)] * 2,
        [((8,) + three, BF16)] * 3 + [((8,) + three, F32)] * 2 + [((2,) + three, BF16)],
        before, first, last, after, metric, w1, w2a, g1, g2,
    )
    return p1, p2, (d, s, de, se, w1a)


def field_part(e, parts):
    c, n, lat = e.shape
    d, s, de, se, w1a = parts
    (out,) = call(
        field_kernel,
        [((c, n, lat), BF16)],
        [((n + 2, 3 * c, lat), BF16)] * 2
        + [((n + 2, c, lat), F32), ((n + 2, 2 * c, lat), F32), ((c * n * lat // 128, 128), F32)],
        e, d, s, de, se, w1a,
    )
    return out


def sum_everywhere(one, two, factor):
    dp, lon = lax.axis_size("dp"), lax.axis_size("lon")
    count = dp * lon
    if (dp & (dp - 1)) or (lon & (lon - 1)) or lon < 2:
        one, two = lax.psum((one.astype(F32), two.astype(F32)), ("dp", "lon"))
        return (one * factor).astype(BF16), (two * factor).astype(BF16)
    odd = lax.axis_index("lon") % 2 == 1
    swap = [(i, i ^ 1) for i in range(count)]
    kept = jnp.where(odd, two, one)
    got = exchange(jnp.where(odd, one, two), swap)
    total = kept.astype(F32) + got.astype(F32)
    inner = [1 << k for k in range(1, lon.bit_length() - 1)]
    outer = [lon << k for k in range(dp.bit_length() - 1)]
    bits = []
    while inner or outer:
        if outer:
            bits.append(outer.pop(0))
        if inner:
            bits.append(inner.pop())
    other = list(bits)
    for k in range(0, len(bits) - 1, 2):
        other[k], other[k + 1] = bits[k + 1], bits[k]
    for even_bit, odd_bit in zip(bits, other):
        sent = total.astype(BF16)
        got = exchange(sent, [(i, i ^ (odd_bit if i & 1 else even_bit)) for i in range(count)])
        total = sent.astype(F32) + got.astype(F32)
    mine = (total * factor).astype(BF16)
    theirs = exchange(mine, swap)
    return jnp.where(odd, theirs, mine), jnp.where(odd, mine, theirs)


def per_device(fields, cotangent, kernel_first, kernel_second, metric):
    samples, c, n, lat = fields.shape
    counted = (
        float(samples * lax.axis_size("dp")) * float(n * lax.axis_size("lon")) * float(lat)
    )
    factor = jnp.float32(1.0 / counted**0.5)
    row = metric.reshape(1, lat)
    one = two = None
    later = []
    for b in range(samples):
        p1, p2, parts = one_sample(fields[b], cotangent[b], kernel_first, kernel_second, row)
        later.append(parts)
        one = p1 if one is None else (one.astype(F32) + p1.astype(F32)).astype(BF16)
        two = p2 if two is None else (two.astype(F32) + p2.astype(F32)).astype(BF16)
    one, two = sum_everywhere(one, two, factor)
    field_grad = jnp.stack([field_part(cotangent[b], later[b]) for b in range(samples)])
    grad_first, grad_second = call(
        final_kernel, [((3, 3, c, c), BF16)] * 2, [], one, two
    )
    return field_grad, grad_first, grad_second


def solution(mesh):
    placed = (P("dp", None, "lon", None), P("dp", None, "lon", None), P(), P(), P())
    return jax.shard_map(
        per_device,
        mesh=mesh,
        in_specs=placed,
        out_specs=(P("dp", None, "lon", None), P(), P()),
        check_vma=False,
    )
```

```python
import functools
import math

import jax
import jax.numpy as jnp
from jax import lax
from jax.experimental import pallas as pl
from jax.experimental.pallas import tpu as pltpu
from jax.sharding import PartitionSpec as P

gelu_coef = 0.7978845608
F32 = jnp.float32
BF16 = jnp.bfloat16
NT = (((1,), (1,)), ((), ()))


def gelu_pair(u):
    inner = jnp.tanh(gelu_coef * (u + 0.044715 * u * u * u))
    value = 0.5 * u * (1.0 + inner)
    slope = 0.5 * (1.0 + inner) + 0.5 * u * (1.0 - inner * inner) * gelu_coef * (
        1.0 + 3.0 * 0.044715 * u * u
    )
    return value, slope


def neighbours(v):
    lat = v.shape[-1]
    row = lax.broadcasted_iota(jnp.int32, v.shape, 1)
    zero = jnp.zeros_like(v)
    below = jnp.where(row == 0, zero, pltpu.roll(v, 1, 1))
    above = jnp.where(row == lat - 1, zero, pltpu.roll(v, lat - 1, 1))
    return below, above


def dot(a, b):
    return jnp.dot(a, b, preferred_element_type=F32)


def dot_nt(a, b):
    return lax.dot_general(a, b, NT, preferred_element_type=F32)


def put_three(ref, index, v, adjoint):
    channels = v.shape[0]
    v = v.astype(BF16)
    below, above = neighbours(v)
    if adjoint:
        below, above = above, below
    ref[index, 0:channels, :] = below
    ref[index, channels : 2 * channels, :] = v
    ref[index, 2 * channels :, :] = above


def prepare(k_ref, forward_ref, adjoint_ref):
    c = k_ref.shape[-1]
    for p in range(3):
        if forward_ref is not None:
            forward_ref[p * c : (p + 1) * c, :] = jnp.concatenate(
                [k_ref[p, q].astype(F32) for q in range(3)], axis=1
            ).astype(BF16)
        adjoint_ref[p * c : (p + 1) * c, :] = jnp.concatenate(
            [k_ref[p, q].astype(F32).T for q in range(3)], axis=1
        ).astype(BF16)


def spread(i, x, e, metric, x3, e3, s3):
    put_three(x3, i, x, False)
    put_three(e3, i, e, True)
    scaled = (metric * e).astype(BF16).astype(F32)
    put_three(s3, i, scaled, True)


def products(i, w1, w2a, x3, e3, s3, y, z):
    c = x3.shape[1] // 3
    y[i] = dot(w1[...], x3[i])
    z[i, c : 2 * c, :] = dot(w2a[c : 2 * c, :], e3[i])
    sides = dot(jnp.concatenate([w2a[0:c, :], w2a[2 * c :, :]], axis=0), s3[i])
    z[i, 0:c, :] = sides[0:c]
    z[i, 2 * c :, :] = sides[c:]


def middle(i, metric, y, z):
    c = y.shape[1] // 3
    u = y[i, c : 2 * c, :] + metric * (y[i - 1, 0:c, :] + y[i + 1, 2 * c :, :])
    hidden, slope = gelu_pair(u)
    grad = z[i, c : 2 * c, :] + (z[i + 1, 0:c, :] + z[i - 1, 2 * c :, :])
    delta = (grad * slope).astype(BF16).astype(F32)
    return hidden.astype(BF16).astype(F32), delta, (metric * delta).astype(BF16).astype(F32)


def three_rows(plain, scaled, j):
    c = plain.shape[1] // 3
    mid = slice(c, 2 * c)
    return jnp.concatenate(
        [scaled[j + 1, mid, :], plain[j, mid, :], scaled[j - 1, mid, :]], axis=0
    )


def scatter_out(ref, value):
    c, n, lat = value.shape
    value = value.astype(F32).reshape(c * n, lat)
    for k in range(lat // 128):
        ref[k * c * n : (k + 1) * c * n, :] = value[:, k * 128 : (k + 1) * 128]


def strided(ref, i, c, n):
    count = ref.shape[0] // (c * n)
    return [(k, pl.ds(k * c * n + i, c, stride=n)) for k in range(count)]


def column(ref, i, c, n):
    return jnp.concatenate([ref[at, :] for _, at in strided(ref, i, c, n)], axis=1)


def interior_kernel(
    x_ref, e_ref, k1_ref, k2_ref, m_ref,
    g1_ref, g2_ref, d_ref, s_ref, w1_ref, w1a_ref, w2a_ref,
    xf, ef, x3, e3, s3, y, z, h3,
):
    c, n, lat = x_ref.shape
    metric = m_ref[...]
    prepare(k1_ref, w1_ref, w1a_ref)
    prepare(k2_ref, None, w2a_ref)
    scatter_out(xf, x_ref[...])
    scatter_out(ef, e_ref[...])

    blank = jnp.zeros((c, lat), BF16)
    for i in (0, n - 1):
        d_ref[i] = blank
        s_ref[i] = blank
    g1_ref[...] = jnp.zeros_like(g1_ref)
    g2_ref[...] = jnp.zeros_like(g2_ref)

    def second_terms(columns):
        left = jnp.concatenate([three_rows(e3, s3, j) for j in columns], axis=1)
        g2_ref[...] += dot_nt(left, jnp.concatenate([h3[j] for j in columns], axis=1))

    def first_terms(columns):
        left = [
            jnp.concatenate([s_ref[j + 1], d_ref[j], s_ref[j - 1]], axis=0) for j in columns
        ]
        right = jnp.concatenate([x3[j] for j in columns], axis=1)
        g1_ref[...] += dot_nt(jnp.concatenate(left, axis=1), right)

    inner = list(range(1, n - 1))
    groups = [inner[k : k + 7] for k in range(0, n - 2, 7)]
    second_todo, first_todo = list(groups), list(groups)
    for i in range(n + 1):
        if i < n:
            spread(i, column(xf, i, c, n), column(ef, i, c, n), metric, x3, e3, s3)
            products(i, w1_ref, w2a_ref, x3, e3, s3, y, z)
        if 1 <= i - 1 < n - 1:
            hidden, delta, scaled = middle(i - 1, metric, y, z)
            put_three(h3, i - 1, hidden, False)
            d_ref[i - 1] = delta.astype(BF16)
            s_ref[i - 1] = scaled.astype(BF16)
        if i == 3:
            g1_ref[0:c, :] += dot_nt(s_ref[1], x3[0])
        ready = i - 2 if i < n else n - 2
        if second_todo and second_todo[0][-1] <= ready:
            second_terms(second_todo.pop(0))
        if first_todo and first_todo[0][-1] <= (ready - 1 if i < n else ready):
            first_terms(first_todo.pop(0))
    for columns in second_todo:
        second_terms(columns)
    for columns in first_todo:
        first_terms(columns)
    g1_ref[2 * c :, :] += dot_nt(s_ref[n - 2], x3[n - 1])


def edge_kernel(
    before_ref, first_ref, last_ref, after_ref, m_ref, w1_ref, w2a_ref, g1_in, g2_in,
    kept_ref, sent_ref, d_ref, s_ref,
    x3, e3, s3, y, z, h3,
):
    metric = m_ref[...]
    c = before_ref.shape[2]
    total1, total2 = g1_in[...], g2_in[...]
    for side, pair in ((0, (before_ref, first_ref)), (1, (last_ref, after_ref))):
        base = 4 * side
        for k in range(4):
            source = pair[k // 2]
            spread(
                base + k, source[0, k % 2].astype(F32), source[1, k % 2].astype(F32), metric, x3, e3, s3
            )
            products(base + k, w1_ref, w2a_ref, x3, e3, s3, y, z)
        own = 2 if side == 0 else 1
        for k in (1, 2):
            hidden, delta, scaled = middle(base + k, metric, y, z)
            d_ref[2 * side + k - 1] = delta.astype(BF16)
            s_ref[2 * side + k - 1] = scaled.astype(BF16)
            if k == own:
                put_three(h3, side, hidden, False)
        j = base + own
        total2 = total2 + dot_nt(three_rows(e3, s3, j), h3[side])
        delta, scaled = d_ref[2 * side + own - 1], s_ref[2 * side + own - 1]
        total1 = total1 + jnp.concatenate(
            [dot_nt(scaled, x3[j - 1]), dot_nt(delta, x3[j]), dot_nt(scaled, x3[j + 1])], axis=0
        )
    odd = lax.axis_index("lon") % 2 == 1
    for ref, total in (
        (kept_ref, jnp.where(odd, total2, total1)),
        (sent_ref, jnp.where(odd, total1, total2)),
    ):
        half = total.shape[0] // 2
        tail = total[:, 2 * c :]
        ref[0 : 2 * half, :] = total[:, 0 : 2 * c].astype(ref.dtype)
        ref[2 * half :, :] = jnp.concatenate([tail[0:half], tail[half:]], axis=1).astype(ref.dtype)


def field_kernel(d_in, s_in, de_ref, se_ref, w1a_ref, out_ref, d3, s3, zm, zs, *, start):
    c, n = d_in.shape[1], d_in.shape[0]
    count = out_ref.shape[0]
    sides = jnp.concatenate([w1a_ref[0:c, :], w1a_ref[2 * c :, :]], axis=0)
    edges = {-1: 0, 0: 1, n - 1: 2, n: 3}
    for place in range(count + 2):
        i = start + place - 1
        d, s = (de_ref[edges[i]], se_ref[edges[i]]) if i in edges else (d_in[i], s_in[i])
        put_three(d3, place, d, True)
        put_three(s3, place, s, True)
        zm[place] = dot(w1a_ref[c : 2 * c, :], d3[place])
        zs[place] = dot(sides, s3[place])
        if place >= 2:
            out_ref[place - 2] = zm[place - 1] + (zs[place, 0:c, :] + zs[place - 2, c:, :])


def assemble_kernel(*refs):
    e_ref, parts, out_ref, ef = refs[0], refs[1:-2], refs[-2], refs[-1]
    c, n, lat = e_ref.shape
    scatter_out(ef, e_ref[...])
    i = 0
    for part in parts:
        for k in range(part.shape[0]):
            grad = part[k]
            for t, at in strided(ef, i, c, n):
                ef[at, :] = ef[at, :] + grad[:, t * 128 : (t + 1) * 128]
            i += 1
    for k in range(lat // 128):
        part = ef[k * c * n : (k + 1) * c * n, :].reshape(c, n, 128)
        out_ref[:, :, k * 128 : (k + 1) * 128] = part.astype(BF16)


def final_kernel(mine_ref, theirs_ref, out1_ref, out2_ref):
    c = out1_ref.shape[-1]
    odd = lax.axis_index("lon") % 2 == 1
    mine, theirs = mine_ref[...], theirs_ref[...]
    for out, packed in (
        (out1_ref, jnp.where(odd, theirs, mine)),
        (out2_ref, jnp.where(odd, mine, theirs)),
    ):
        tail = packed[3 * c :]
        tail = jnp.concatenate([tail[:, 0:c], tail[:, c:]], axis=0)
        for p in range(3):
            rows = slice(p * c, (p + 1) * c)
            out[p, 0] = packed[rows, 0:c]
            out[p, 1] = packed[rows, c:]
            out[p, 2] = tail[rows]


def vmem(count):
    return [pl.BlockSpec(memory_space=pltpu.VMEM)] * count


def size_of(shapes):
    return sum(math.prod(s) * jnp.dtype(d).itemsize for s, d in shapes)


def call(kernel, outs, scratch, *args):
    mib = 2**20
    limit = size_of(scratch) + size_of(outs) + size_of([(a.shape, a.dtype) for a in args])
    return pl.pallas_call(
        kernel,
        out_shape=[jax.ShapeDtypeStruct(s, d) for s, d in outs],
        in_specs=vmem(len(args)),
        out_specs=vmem(len(outs)),
        scratch_shapes=[pltpu.VMEM(s, d) for s, d in scratch],
        compiler_params=pltpu.CompilerParams(vmem_limit_bytes=(limit // mib + 6) * mib),
    )(*args)


def exchange(value, pairs):
    return lax.ppermute(value, ("dp", "lon"), pairs)


def one_sample(x, e, kernel_first, kernel_second, metric):
    c, n, lat = x.shape
    wide = 3 * c
    size = lax.axis_size("lon")
    up = [(i, (i + 1) % size) for i in range(size)]
    down = [(j, i) for i, j in up]
    first = jnp.swapaxes(jnp.stack((x[:, 0:2], e[:, 0:2])), 1, 2)
    last = jnp.swapaxes(jnp.stack((x[:, n - 2 :], e[:, n - 2 :])), 1, 2)
    before = lax.ppermute(last, "lon", up)
    after = lax.ppermute(first, "lon", down)
    three = (wide, lat)
    g1, g2, d, s, w1, w1a, w2a = call(
        interior_kernel,
        [((wide, wide), F32)] * 2 + [((n, c, lat), BF16)] * 2 + [((wide, wide), BF16)] * 3,
        [((c * n * lat // 128, 128), F32)] * 2
        + [((n,) + three, BF16)] * 3
        + [((n,) + three, F32)] * 2
        + [((n,) + three, BF16)],
        x, e, kernel_first, kernel_second, metric,
    )
    packed = (3 * wide // 2, 2 * c)
    kept, sent, de, se = call(
        edge_kernel,
        [(packed, F32), (packed, BF16)] + [((4, c, lat), BF16)] * 2,
        [((8,) + three, BF16)] * 3 + [((8,) + three, F32)] * 2 + [((2,) + three, BF16)],
        before, first, last, after, metric, w1, w2a, g1, g2,
    )
    return kept, sent, (d, s, de, se, w1a)


def field_parts(parts, pieces):
    n, c, lat = parts[0].shape
    wide = 3 * c
    made, start = [], 0
    for k in range(pieces):
        stop = n * (k + 1) // pieces
        count = stop - start
        made.append(
            functools.partial(
                call,
                functools.partial(field_kernel, start=start),
                [((count, c, lat), F32)],
                [((count + 2, wide, lat), BF16)] * 2
                + [((count + 2, c, lat), F32), ((count + 2, 2 * c, lat), F32)],
                *parts,
            )
        )
        start = stop
    return made


def assemble(e, grads):
    c, n, lat = e.shape
    return call(
        assemble_kernel, [((c, n, lat), BF16)], [((c * n * lat // 128, 128), F32)], e, *grads
    )[0]


def sum_everywhere(kept, sent, factor, jobs):
    dp, lon = lax.axis_size("dp"), lax.axis_size("lon")
    count = dp * lon
    swap = [(i, i ^ 1) for i in range(count)]
    total = kept + exchange(sent, swap).astype(F32)
    inner = [1 << k for k in range(1, lon.bit_length() - 1)]
    outer = [lon << k for k in range(dp.bit_length() - 1)]
    bits = []
    while inner or outer:
        if outer:
            bits.append(outer.pop(0))
        if inner:
            bits.append(inner.pop())
    other = list(bits)
    for k in range(0, len(bits) - 1, 2):
        other[k], other[k + 1] = bits[k + 1], bits[k]
    results = []
    for even_bit, odd_bit in zip(bits, other):
        sent = total.astype(BF16)
        got = exchange(sent, [(i, i ^ (odd_bit if i & 1 else even_bit)) for i in range(count)])
        if jobs:
            sent, job_args = lax.optimization_barrier((sent, jobs[0][1](results)))
            results.append(jobs.pop(0)[0](*job_args))
            got, results[-1] = lax.optimization_barrier((got, results[-1]))
        total = sent.astype(F32) + got.astype(F32)
    for job in jobs:
        results.append(job[0](*job[1](results)))
    mine = (total * factor).astype(BF16)
    return mine, exchange(mine, swap), results


def per_device(fields, cotangent, kernel_first, kernel_second, metric):
    samples, c, n, lat = fields.shape
    counted = (
        float(samples * lax.axis_size("dp")) * float(n * lax.axis_size("lon")) * float(lat)
    )
    factor = jnp.float32(1.0 / counted**0.5)
    row = metric.reshape(1, lat)
    kept = sent = None
    jobs = []
    pieces = 2
    for b in range(samples):
        k, t, parts = one_sample(fields[b], cotangent[b], kernel_first, kernel_second, row)
        kept = k if kept is None else kept + k
        sent = t if sent is None else (sent.astype(F32) + t.astype(F32)).astype(BF16)
        for job in field_parts(parts, pieces):
            jobs.append((lambda *args, job=job: job.func(*job.args[:3], *args)[0], lambda done, job=job: job.args[3:]))
        jobs.append((
            lambda *args: assemble(args[0], args[1:]),
            lambda done, b=b: (cotangent[b],) + tuple(done[-pieces:]),
        ))
    mine, theirs, results = sum_everywhere(kept, sent, factor, jobs)
    field_grad = jnp.stack(results[pieces :: pieces + 1])
    grad_first, grad_second = call(
        final_kernel, [((3, 3, c, c), BF16)] * 2, [], mine, theirs
    )
    return field_grad, grad_first, grad_second


def solution(mesh):
    placed = (P("dp", None, "lon", None), P("dp", None, "lon", None), P(), P(), P())
    return jax.shard_map(
        per_device,
        mesh=mesh,
        in_specs=placed,
        out_specs=(P("dp", None, "lon", None), P(), P()),
        check_vma=False,
    )
```

```python
import functools
import math

import jax
import jax.numpy as jnp
from jax import lax
from jax.experimental import pallas as pl
from jax.experimental.pallas import tpu as pltpu
from jax.sharding import PartitionSpec as P

gelu_coef = 0.7978845608
F32 = jnp.float32
BF16 = jnp.bfloat16
NT = (((1,), (1,)), ((), ()))


def gelu_pair(u):
    inner = jnp.tanh(gelu_coef * (u + 0.044715 * u * u * u))
    value = 0.5 * u * (1.0 + inner)
    slope = 0.5 * (1.0 + inner) + 0.5 * u * (1.0 - inner * inner) * gelu_coef * (
        1.0 + 3.0 * 0.044715 * u * u
    )
    return value, slope


def neighbours(v):
    lat = v.shape[-1]
    row = lax.broadcasted_iota(jnp.int32, v.shape, 1)
    zero = jnp.zeros_like(v)
    below = jnp.where(row == 0, zero, pltpu.roll(v, 1, 1))
    above = jnp.where(row == lat - 1, zero, pltpu.roll(v, lat - 1, 1))
    return below, above


def dot(a, b):
    return jnp.dot(a, b, preferred_element_type=F32)


def dot_nt(a, b):
    return lax.dot_general(a, b, NT, preferred_element_type=F32)


def put_three(ref, index, v, adjoint):
    channels = v.shape[0]
    v = v.astype(BF16)
    below, above = neighbours(v)
    if adjoint:
        below, above = above, below
    ref[index, 0:channels, :] = below
    ref[index, channels : 2 * channels, :] = v
    ref[index, 2 * channels :, :] = above


def prepare(k_ref, forward_ref, adjoint_ref):
    c = k_ref.shape[-1]
    for p in range(3):
        if forward_ref is not None:
            forward_ref[p * c : (p + 1) * c, :] = jnp.concatenate(
                [k_ref[p, q].astype(F32) for q in range(3)], axis=1
            ).astype(BF16)
        adjoint_ref[p * c : (p + 1) * c, :] = jnp.concatenate(
            [k_ref[p, q].astype(F32).T for q in range(3)], axis=1
        ).astype(BF16)


class Columns:
    def __init__(self, place):
        self.place = place

    def __getitem__(self, at):
        i, rest = (at[0], at[1:]) if isinstance(at, tuple) else (at, ())
        ref, k = self.place[i]
        return ref[(k,) + rest]

    def __setitem__(self, at, value):
        i, rest = (at[0], at[1:]) if isinstance(at, tuple) else (at, ())
        ref, k = self.place[i]
        ref[(k,) + rest] = value


def split(outside, edges, inside):
    return Columns(
        {i: (outside, edges.index(i)) if i in edges else (inside, i) for i in range(inside.shape[0])}
    )


def spread(i, x, e, metric, x3, e3, s3):
    put_three(x3, i, x, False)
    put_three(e3, i, e, True)
    scaled = (metric * e).astype(BF16)
    put_three(s3, i, scaled, True)


def products(i, w1, w2a, x3, e3, s3, y, z):
    c = w1.shape[0] // 3
    y[i] = dot(w1[...], x3[i])
    z[i, c : 2 * c, :] = dot(w2a[c : 2 * c, :], e3[i])
    sides = dot(jnp.concatenate([w2a[0:c, :], w2a[2 * c :, :]], axis=0), s3[i])
    z[i, 0:c, :] = sides[0:c]
    z[i, 2 * c :, :] = sides[c:]


def middle(i, metric, y, z):
    c = z[i].shape[0] // 3
    u = y[i, c : 2 * c, :] + metric * (y[i - 1, 0:c, :] + y[i + 1, 2 * c :, :])
    hidden, slope = gelu_pair(u)
    grad = z[i, c : 2 * c, :] + (z[i + 1, 0:c, :] + z[i - 1, 2 * c :, :])
    delta = (grad * slope).astype(BF16)
    return hidden.astype(BF16), delta, (metric * delta.astype(F32)).astype(BF16)


def three_rows(plain, scaled, j):
    c = plain[j].shape[0] // 3
    mid = slice(c, 2 * c)
    return jnp.concatenate(
        [scaled[j + 1, mid, :], plain[j, mid, :], scaled[j - 1, mid, :]], axis=0
    )


def scatter_out(ref, value, first=0):
    c, n, lat = value.shape
    value = value.astype(F32).reshape(c * n, lat)
    whole = ref.shape[0] * 128 // lat
    for k in range(lat // 128):
        at = k * whole + first
        ref[at : at + c * n, :] = value[:, k * 128 : (k + 1) * 128]


def strided(ref, i, c, n):
    count = ref.shape[0] // (c * n)
    return [(k, pl.ds(k * c * n + i, c, stride=n)) for k in range(count)]


def column(ref, i, c, n):
    return jnp.concatenate([ref[at, :] for _, at in strided(ref, i, c, n)], axis=1)


def pack_kernel(
    x_hbm, e_hbm, m_hbm, xf, ef, mate_ref, outer_ref, row_ref, xs, es, ms, sems, row_sem
):
    c, n, lat = x_hbm.shape
    chunks = sems.shape[1]
    w = c // chunks
    copies = []
    for k in range(chunks):
        for a, (src, dst) in enumerate(((x_hbm, xs), (e_hbm, es))):
            rows = pl.ds(k * w, w)
            copies.append(pltpu.make_async_copy(src.at[rows], dst.at[rows], sems.at[a, k]))
            copies[-1].start()
    row_copy = pltpu.make_async_copy(m_hbm, ms, row_sem)
    row_copy.start()
    for k in range(chunks):
        for a, (src, dst) in enumerate(((xs, xf), (es, ef))):
            copies[2 * k + a].wait()
            scatter_out(dst, src[k * w : (k + 1) * w], k * w * n)
    odd = lax.axis_index("lon") % 2 == 1
    for a, source in enumerate((xf, ef)):
        for k in range(2):
            low = column(source, k, c, n).astype(BF16)
            high = column(source, n - 2 + k, c, n).astype(BF16)
            mate_ref[a, k] = jnp.where(odd, low, high)
            outer_ref[a, k] = jnp.where(odd, high, low)
    row_copy.wait()
    row_ref[...] = ms[...].reshape(1, lat)


def interior_kernel(
    xf, ef, k1_ref, k2_ref, m_ref,
    g1_ref, g2_ref, d_ref, s_ref, w1_ref, w1a_ref, w2a_ref, x3_out, e3_out, s3_out, y_out, z_out,
    x3_in, e3_in, s3_in, y_in, z_in, h3,
):
    n, c, lat = d_ref.shape
    metric = m_ref[...]
    prepare(k1_ref, w1_ref, w1a_ref)
    prepare(k2_ref, None, w2a_ref)
    edges = (0, 1, n - 2, n - 1)
    x3, e3, s3, y, z = (
        split(outside, edges, inside)
        for outside, inside in (
            (x3_out, x3_in), (e3_out, e3_in), (s3_out, s3_in), (y_out, y_in), (z_out, z_in)
        )
    )
    blank = jnp.zeros((c, lat), BF16)
    for i in (0, n - 1):
        d_ref[i] = blank
        s_ref[i] = blank
    g1_ref[...] = jnp.zeros_like(g1_ref)
    g2_ref[...] = jnp.zeros_like(g2_ref)

    def second_terms(columns):
        left = jnp.concatenate([three_rows(e3, s3, j) for j in columns], axis=1)
        g2_ref[...] += dot_nt(left, jnp.concatenate([h3[j] for j in columns], axis=1))

    def first_terms(columns):
        left = [
            jnp.concatenate([s_ref[j + 1], d_ref[j], s_ref[j - 1]], axis=0) for j in columns
        ]
        right = jnp.concatenate([x3[j] for j in columns], axis=1)
        g1_ref[...] += dot_nt(jnp.concatenate(left, axis=1), right)

    inner = list(range(1, n - 1))
    groups = [inner[k : k + 7] for k in range(0, n - 2, 7)]
    second_todo, first_todo = list(groups), list(groups)
    for i in range(n + 1):
        if i < n:
            spread(i, column(xf, i, c, n), column(ef, i, c, n), metric, x3, e3, s3)
            products(i, w1_ref, w2a_ref, x3, e3, s3, y, z)
        if 1 <= i - 1 < n - 1:
            hidden, delta, scaled = middle(i - 1, metric, y, z)
            put_three(h3, i - 1, hidden, False)
            d_ref[i - 1] = delta
            s_ref[i - 1] = scaled
        if i == 3:
            g1_ref[0:c, :] += dot_nt(s_ref[1], x3[0])
        ready = i - 2 if i < n else n - 2
        if second_todo and second_todo[0][-1] <= ready:
            second_terms(second_todo.pop(0))
        if first_todo and first_todo[0][-1] <= (ready - 1 if i < n else ready):
            first_terms(first_todo.pop(0))
    for columns in second_todo:
        second_terms(columns)
    for columns in first_todo:
        first_terms(columns)
    g1_ref[2 * c :, :] += dot_nt(s_ref[n - 2], x3[n - 1])


def parity():
    place = lax.axis_index("dp") * lax.axis_size("lon") + lax.axis_index("lon")
    total, left = 0, lax.axis_size("dp") * lax.axis_size("lon") - 1
    while left:
        total, place, left = total + place % 2, place // 2, left // 2
    return total % 2


def edge_kernel(
    to_mate, to_outer, from_mate, from_outer, m_ref, w1, w2a, g1_in, g2_in, x3_own, e3_own, s3_own, y_own, z_own,
    kept_ref, sent_ref, d_ref, s_ref,
    x3_far, e3_far, s3_far, y_far, z_far, h3,
):
    metric = m_ref[...]
    c = to_mate.shape[2]
    odd = lax.axis_index("lon") % 2 == 1
    low, mid, high = slice(0, c), slice(c, 2 * c), slice(2 * c, 3 * c)
    far, own = (0, 1, 6, 7), (2, 3, 4, 5)

    def both(outside, inside):
        places = {i: (outside, k) for k, i in enumerate(far)}
        places.update({i: (inside, k) for k, i in enumerate(own)})
        return Columns(places)

    x3, e3, s3, y, z = (
        both(*pair)
        for pair in (
            (x3_far, x3_own), (e3_far, e3_own), (s3_far, s3_own), (y_far, y_own), (z_far, z_own)
        )
    )
    total1, total2 = g1_in[...], g2_in[...]
    for side in range(2):
        base = 4 * side
        for k in range(2):
            i = base + 2 * side + k
            x, e = (
                jnp.where(odd, from_outer[a, k], from_mate[a, k])
                if side
                else jnp.where(odd, from_mate[a, k], from_outer[a, k])
                for a in range(2)
            )
            put_three(x3, i, x, False)
            scaled = (metric * e.astype(F32)).astype(BF16)
            put_three(s3, i, scaled, True)
            near = k != side
            one, two = (high, low) if side else (low, high)
            y[i, one, :] = dot(w1[one, :], x3[i])
            z[i, two, :] = dot(w2a[two, :], s3[i])
            if near:
                put_three(e3, i, e, True)
                y[i, mid, :] = dot(w1[mid, :], x3[i])
                z[i, mid, :] = dot(w2a[mid, :], e3[i])
        for k in (1, 2):
            hidden, delta, scaled = middle(base + k, metric, y, z)
            d_ref[2 * side + k - 1] = delta
            s_ref[2 * side + k - 1] = scaled
            if k == 2 - side:
                put_three(h3, side, hidden, False)
                j = base + k
                total2 = total2 + dot_nt(three_rows(e3, s3, j), h3[side])
                total1 = total1 + jnp.concatenate(
                    [dot_nt(scaled, x3[j - 1]), dot_nt(delta, x3[j]), dot_nt(scaled, x3[j + 1])],
                    axis=0,
                )
    keeps_second = parity() == 1
    for ref, total in (
        (kept_ref, jnp.where(keeps_second, total2, total1)),
        (sent_ref, jnp.where(keeps_second, total1, total2)),
    ):
        half = total.shape[0] // 2
        tail = total[:, 2 * c :]
        ref[0 : 2 * half, :] = total[:, 0 : 2 * c].astype(ref.dtype)
        ref[2 * half :, :] = jnp.concatenate([tail[0:half], tail[half:]], axis=1).astype(ref.dtype)


def field_kernel(d_in, s_in, de_ref, se_ref, w1a_ref, out_ref, d3, s3, zm, zs, *, start):
    c, n = d_in.shape[1], d_in.shape[0]
    count = out_ref.shape[0]
    sides = jnp.concatenate([w1a_ref[0:c, :], w1a_ref[2 * c :, :]], axis=0)
    edges = {-1: 0, 0: 1, n - 1: 2, n: 3}
    for place in range(count + 2):
        i = start + place - 1
        d, s = (de_ref[edges[i]], se_ref[edges[i]]) if i in edges else (d_in[i], s_in[i])
        put_three(d3, place, d, True)
        put_three(s3, place, s, True)
        zm[place] = dot(w1a_ref[c : 2 * c, :], d3[place])
        zs[place] = dot(sides, s3[place])
        if place >= 2:
            out_ref[place - 2] = zm[place - 1] + (zs[place, 0:c, :] + zs[place - 2, c:, :])


def assemble_kernel(*refs):
    e_ref, parts, out_ref, ef = refs[0], refs[1:-2], refs[-2], refs[-1]
    c, n, lat = out_ref.shape
    i = 0
    for part in parts:
        for k in range(part.shape[0]):
            grad = part[k]
            for t, at in strided(ef, i, c, n):
                ef[at, :] = e_ref[at, :] + grad[:, t * 128 : (t + 1) * 128]
            i += 1
    for k in range(lat // 128):
        part = ef[k * c * n : (k + 1) * c * n, :].reshape(c, n, 128)
        out_ref[:, :, k * 128 : (k + 1) * 128] = part.astype(BF16)


def final_kernel(mine_ref, theirs_ref, out1_ref, out2_ref):
    c = out1_ref.shape[-1]
    odd = parity() == 1
    mine, theirs = mine_ref[...], theirs_ref[...]
    for out, packed in (
        (out1_ref, jnp.where(odd, theirs, mine)),
        (out2_ref, jnp.where(odd, mine, theirs)),
    ):
        tail = packed[3 * c :]
        tail = jnp.concatenate([tail[:, 0:c], tail[:, c:]], axis=0)
        for p in range(3):
            rows = slice(p * c, (p + 1) * c)
            out[p, 0] = packed[rows, 0:c]
            out[p, 1] = packed[rows, c:]
            out[p, 2] = tail[rows]


def vmem(count):
    return [pl.BlockSpec(memory_space=pltpu.VMEM)] * count


def size_of(shapes):
    return sum(math.prod(s) * jnp.dtype(d).itemsize for s, d in shapes)


def call(kernel, outs, scratch, *args, specs=None):
    mib = 2**20
    buffers = [s for s in scratch if isinstance(s, tuple)]
    limit = size_of(buffers) + size_of(outs) + size_of([(a.shape, a.dtype) for a in args])
    return pl.pallas_call(
        kernel,
        out_shape=[jax.ShapeDtypeStruct(s, d) for s, d in outs],
        in_specs=specs or vmem(len(args)),
        out_specs=vmem(len(outs)),
        scratch_shapes=[pltpu.VMEM(*s) if isinstance(s, tuple) else s for s in scratch],
        compiler_params=pltpu.CompilerParams(vmem_limit_bytes=(limit // mib + 6) * mib),
    )(*args)


def exchange(value, pairs):
    return lax.ppermute(value, ("dp", "lon"), pairs)


def one_sample(x, e, kernel_first, kernel_second, metric):
    c, n, lat = x.shape
    wide = 3 * c
    chunks = 4
    count = lax.axis_size("dp") * lax.axis_size("lon")
    lon = lax.axis_size("lon")
    mates = [(i, i ^ 1) for i in range(count)]
    outers = [
        (i, i // lon * lon + (i % lon + (1 if i % lon % 2 else -1)) % lon) for i in range(count)
    ]
    strided_form = ((c * n * lat // 128, 128), F32)
    column = (wide, lat)
    halo = ((2, 2, c, lat), BF16)
    copied = [pl.BlockSpec(memory_space=pltpu.HBM)] * 3
    xf, ef, to_mate, to_outer, row = call(
        pack_kernel,
        [strided_form] * 2 + [halo] * 2 + [((1, lat), F32)],
        [((c, n, lat), BF16)] * 2
        + [((lat,), F32), pltpu.SemaphoreType.DMA((2, chunks)), pltpu.SemaphoreType.DMA],
        *(pltpu.with_memory_space_constraint(a, pltpu.HBM) for a in (x, e, metric)),
        specs=copied,
    )
    from_mate = exchange(to_mate, mates)
    from_outer = exchange(to_outer, outers)
    four = [((4,) + column, BF16)] * 3 + [((4,) + column, F32)] * 2
    square = (wide, wide)
    g1, g2, d, s, w1, w1a, w2a, *own = call(
        interior_kernel,
        [(square, F32)] * 2 + [((n, c, lat), BF16)] * 2 + [(square, BF16)] * 3 + four,
        [((n,) + column, BF16)] * 3 + [((n,) + column, F32)] * 2 + [((n,) + column, BF16)],
        xf, ef, kernel_first, kernel_second, row,
    )
    packed = (3 * wide // 2, 2 * c)
    kept, sent, de, se = call(
        edge_kernel,
        [(packed, F32), (packed, BF16)] + [((4, c, lat), BF16)] * 2,
        four + [((2,) + column, BF16)],
        to_mate, to_outer, from_mate, from_outer, row, w1, w2a, g1, g2, *own,
    )
    return kept, sent, (d, s, de, se, w1a), ef


def field_parts(parts, pieces):
    n, c, lat = parts[0].shape
    wide = 3 * c
    made, start = [], 0
    for k in range(pieces):
        stop = n * (k + 1) // pieces
        count = stop - start
        made.append(
            functools.partial(
                call,
                functools.partial(field_kernel, start=start),
                [((count, c, lat), F32)],
                [((count + 2, wide, lat), BF16)] * 2
                + [((count + 2, c, lat), F32), ((count + 2, 2 * c, lat), F32)],
                *parts,
            )
        )
        start = stop
    return made


def assemble(e, grads):
    n = sum(g.shape[0] for g in grads)
    _, c, lat = grads[0].shape
    return call(
        assemble_kernel, [((c, n, lat), BF16)], [((c * n * lat // 128, 128), F32)], e, *grads
    )[0]


def sum_everywhere(kept, sent, factor, jobs):
    dp, lon = lax.axis_size("dp"), lax.axis_size("lon")
    count = dp * lon
    swap = [(i, i ^ 1) for i in range(count)]
    total = kept + exchange(sent, swap).astype(F32)
    inner = [1 << k for k in range(1, lon.bit_length() - 1)]
    outer = [lon << k for k in range(dp.bit_length() - 1)]
    bits = []
    while inner or outer:
        if outer:
            bits.append(outer.pop(0))
        if inner:
            bits.append(inner.pop())
    other = list(bits)
    for k in range(0, len(bits) - 1, 2):
        other[k], other[k + 1] = bits[k + 1], bits[k]
    results = []
    for even_bit, odd_bit in zip(bits, other):
        sent = total.astype(BF16)
        got = exchange(
            sent, [(i, i ^ 1 ^ (odd_bit if i.bit_count() & 1 else even_bit)) for i in range(count)]
        )
        if jobs:
            sent, job_args = lax.optimization_barrier((sent, jobs[0][1](results)))
            results.append(jobs.pop(0)[0](*job_args))
            got, results[-1] = lax.optimization_barrier((got, results[-1]))
        total = sent.astype(F32) + got.astype(F32)
    for job in jobs:
        results.append(job[0](*job[1](results)))
    mine = (total * factor).astype(BF16)
    return mine, exchange(mine, swap), results


def per_device(fields, cotangent, kernel_first, kernel_second, metric):
    samples, c, n, lat = fields.shape
    counted = (
        float(samples * lax.axis_size("dp")) * float(n * lax.axis_size("lon")) * float(lat)
    )
    factor = jnp.float32(1.0 / counted**0.5)
    kept = sent = None
    jobs = []
    pieces = 2
    for b in range(samples):
        k, t, parts, ef = one_sample(fields[b], cotangent[b], kernel_first, kernel_second, metric)
        kept = k if kept is None else kept + k
        sent = t if sent is None else (sent.astype(F32) + t.astype(F32)).astype(BF16)
        for job in field_parts(parts, pieces):
            jobs.append((lambda *args, job=job: job.func(*job.args[:3], *args)[0], lambda done, job=job: job.args[3:]))
        jobs.append((
            lambda *args: assemble(args[0], args[1:]),
            lambda done, ef=ef: (ef,) + tuple(done[-pieces:]),
        ))
    mine, theirs, results = sum_everywhere(kept, sent, factor, jobs)
    field_grad = jnp.stack(results[pieces :: pieces + 1])
    grad_first, grad_second = call(
        final_kernel, [((3, 3, c, c), BF16)] * 2, [], mine, theirs
    )
    return field_grad, grad_first, grad_second


def solution(mesh):
    placed = (P("dp", None, "lon", None), P("dp", None, "lon", None), P(), P(), P())
    return jax.shard_map(
        per_device,
        mesh=mesh,
        in_specs=placed,
        out_specs=(P("dp", None, "lon", None), P(), P()),
        check_vma=False,
    )
```

```python
import functools
import math

import jax
import jax.numpy as jnp
from jax import lax
from jax.experimental import pallas as pl
from jax.experimental.pallas import tpu as pltpu
from jax.sharding import PartitionSpec as P

gelu_coef = 0.7978845608
F32 = jnp.float32
BF16 = jnp.bfloat16
NT = (((1,), (1,)), ((), ()))


def gelu_pair(u):
    square = u * u
    inner = jnp.tanh(u * (gelu_coef + (gelu_coef * 0.044715) * square))
    a = 0.5 + 0.5 * inner
    value = u * a
    twice = 2.0 * gelu_coef + (6.0 * gelu_coef * 0.044715) * square
    return value, a + (value - value * a) * twice


def neighbours(v):
    lanes = 128
    tiles = [v[:, k : k + lanes] for k in range(0, v.shape[-1], lanes)]
    lane = lax.broadcasted_iota(jnp.int32, tiles[0].shape, 1)
    zero = jnp.zeros_like(tiles[0])
    up = [zero] + [pltpu.roll(t, 1, 1) for t in tiles]
    down = [pltpu.roll(t, lanes - 1, 1) for t in tiles] + [zero]
    below = [jnp.where(lane == 0, up[k], up[k + 1]) for k in range(len(tiles))]
    above = [jnp.where(lane == lanes - 1, down[k + 1], down[k]) for k in range(len(tiles))]
    return jnp.concatenate(below, axis=1), jnp.concatenate(above, axis=1)


def dot(a, b):
    return jnp.dot(a, b, preferred_element_type=F32)


def dot_nt(a, b):
    return lax.dot_general(a, b, NT, preferred_element_type=F32)


def put_three(ref, index, v, adjoint):
    channels = v.shape[0]
    v = v.astype(BF16)
    below, above = neighbours(v)
    if adjoint:
        below, above = above, below
    ref[index, 0:channels, :] = below
    ref[index, channels : 2 * channels, :] = v
    ref[index, 2 * channels :, :] = above


def prepare(k_ref, forward_ref, adjoint_ref):
    c = k_ref.shape[-1]
    for p in range(3):
        if forward_ref is not None:
            forward_ref[p * c : (p + 1) * c, :] = jnp.concatenate(
                [k_ref[p, q].astype(F32) for q in range(3)], axis=1
            ).astype(BF16)
        adjoint_ref[p * c : (p + 1) * c, :] = jnp.concatenate(
            [k_ref[p, q].astype(F32).T for q in range(3)], axis=1
        ).astype(BF16)


class Columns:
    def __init__(self, place):
        self.place = place

    def __getitem__(self, at):
        i, rest = (at[0], at[1:]) if isinstance(at, tuple) else (at, ())
        ref, k = self.place[i]
        return ref[(k,) + rest]

    def __setitem__(self, at, value):
        i, rest = (at[0], at[1:]) if isinstance(at, tuple) else (at, ())
        ref, k = self.place[i]
        ref[(k,) + rest] = value


def split(outside, edges, inside):
    return Columns(
        {i: (outside, edges.index(i)) if i in edges else (inside, i) for i in range(inside.shape[0])}
    )


def spread(i, x, e, metric, x3, e3, s3):
    put_three(x3, i, x, False)
    put_three(e3, i, e, True)
    scaled = (metric * e).astype(BF16)
    put_three(s3, i, scaled, True)


def products(i, w1, w2a, x3, e3, s3, y, z):
    c = w1.shape[0] // 3
    y[i] = dot(w1[...], x3[i])
    z[i, c : 2 * c, :] = dot(w2a[c : 2 * c, :], e3[i])
    sides = dot(jnp.concatenate([w2a[0:c, :], w2a[2 * c :, :]], axis=0), s3[i])
    z[i, 0:c, :] = sides[0:c]
    z[i, 2 * c :, :] = sides[c:]


def middle(i, metric, y, z):
    c = z[i].shape[0] // 3
    u = y[i, c : 2 * c, :] + metric * (y[i - 1, 0:c, :] + y[i + 1, 2 * c :, :])
    hidden, slope = gelu_pair(u)
    grad = z[i, c : 2 * c, :] + (z[i + 1, 0:c, :] + z[i - 1, 2 * c :, :])
    delta = (grad * slope).astype(BF16)
    return hidden.astype(BF16), delta, (metric * delta.astype(F32)).astype(BF16)


def three_rows(plain, scaled, j):
    c = plain[j].shape[0] // 3
    mid = slice(c, 2 * c)
    return jnp.concatenate(
        [scaled[j + 1, mid, :], plain[j, mid, :], scaled[j - 1, mid, :]], axis=0
    )


def scatter_out(ref, value, first=0):
    c, n, lat = value.shape
    value = value.astype(F32).reshape(c * n, lat)
    whole = ref.shape[0] * 128 // lat
    for k in range(lat // 128):
        at = k * whole + first
        ref[at : at + c * n, :] = value[:, k * 128 : (k + 1) * 128]


def strided(ref, i, c, n):
    count = ref.shape[0] // (c * n)
    return [(k, pl.ds(k * c * n + i, c, stride=n)) for k in range(count)]


def column(ref, i, c, n):
    return jnp.concatenate([ref[at, :] for _, at in strided(ref, i, c, n)], axis=1)


def pack_kernel(
    x_hbm, e_hbm, m_hbm, k1_hbm, k2_hbm,
    xf, ef, mate_ref, outer_ref, row_ref, w1_ref, w1a_ref, w2a_ref,
    xs, es, ms, k1s, k2s, sems, small_sems,
):
    c, n, lat = x_hbm.shape
    chunks = sems.shape[1]
    w = c // chunks
    small = [
        pltpu.make_async_copy(src, dst, small_sems.at[k])
        for k, (src, dst) in enumerate(((k1_hbm, k1s), (k2_hbm, k2s), (m_hbm, ms)))
    ]
    for copy in small:
        copy.start()
    copies = []
    for k in range(chunks):
        for a, (src, dst) in enumerate(((x_hbm, xs), (e_hbm, es))):
            rows = pl.ds(k * w, w)
            copies.append(pltpu.make_async_copy(src.at[rows], dst.at[rows], sems.at[a, k]))
            copies[-1].start()
    for copy in small:
        copy.wait()
    row_ref[...] = ms[...].reshape(1, lat)
    prepare(k1s, w1_ref, w1a_ref)
    prepare(k2s, None, w2a_ref)
    for k in range(chunks):
        for a, (src, dst) in enumerate(((xs, xf), (es, ef))):
            copies[2 * k + a].wait()
            scatter_out(dst, src[k * w : (k + 1) * w], k * w * n)
    odd = lax.axis_index("lon") % 2 == 1
    for a, source in enumerate((xf, ef)):
        for k in range(2):
            low = column(source, k, c, n).astype(BF16)
            high = column(source, n - 2 + k, c, n).astype(BF16)
            mate_ref[a, k] = jnp.where(odd, low, high)
            outer_ref[a, k] = jnp.where(odd, high, low)


def interior_kernel(
    xf, ef, w1_ref, w2a_ref, m_ref,
    g1_ref, g2_ref, d_ref, s_ref, x3_out, e3_out, s3_out, y_out, z_out,
    x3_in, e3_in, s3_in, y_in, z_in, h3,
):
    n, c, lat = d_ref.shape
    metric = m_ref[...]
    edges = (0, 1, n - 2, n - 1)
    x3, e3, s3, y, z = (
        split(outside, edges, inside)
        for outside, inside in (
            (x3_out, x3_in), (e3_out, e3_in), (s3_out, s3_in), (y_out, y_in), (z_out, z_in)
        )
    )
    blank = jnp.zeros((c, lat), BF16)
    for i in (0, n - 1):
        d_ref[i] = blank
        s_ref[i] = blank
    g1_ref[...] = jnp.zeros_like(g1_ref)
    g2_ref[...] = jnp.zeros_like(g2_ref)

    def second_terms(columns):
        left = jnp.concatenate([three_rows(e3, s3, j) for j in columns], axis=1)
        g2_ref[...] += dot_nt(left, jnp.concatenate([h3[j] for j in columns], axis=1))

    def first_terms(columns):
        left = [
            jnp.concatenate([s_ref[j + 1], d_ref[j], s_ref[j - 1]], axis=0) for j in columns
        ]
        right = jnp.concatenate([x3[j] for j in columns], axis=1)
        g1_ref[...] += dot_nt(jnp.concatenate(left, axis=1), right)

    inner = list(range(1, n - 1))
    groups = [inner[k : k + 7] for k in range(0, n - 2, 7)]
    second_todo, first_todo = list(groups), list(groups)
    for i in range(n + 1):
        if i < n:
            spread(i, column(xf, i, c, n), column(ef, i, c, n), metric, x3, e3, s3)
            products(i, w1_ref, w2a_ref, x3, e3, s3, y, z)
        if 1 <= i - 1 < n - 1:
            hidden, delta, scaled = middle(i - 1, metric, y, z)
            put_three(h3, i - 1, hidden, False)
            d_ref[i - 1] = delta
            s_ref[i - 1] = scaled
        if i == 3:
            g1_ref[0:c, :] += dot_nt(s_ref[1], x3[0])
        ready = i - 2 if i < n else n - 2
        if second_todo and second_todo[0][-1] <= ready:
            second_terms(second_todo.pop(0))
        if first_todo and first_todo[0][-1] <= (ready - 1 if i < n else ready):
            first_terms(first_todo.pop(0))
    for columns in second_todo:
        second_terms(columns)
    for columns in first_todo:
        first_terms(columns)
    g1_ref[2 * c :, :] += dot_nt(s_ref[n - 2], x3[n - 1])


def parity():
    place = lax.axis_index("dp") * lax.axis_size("lon") + lax.axis_index("lon")
    total, left = 0, lax.axis_size("dp") * lax.axis_size("lon") - 1
    while left:
        total, place, left = total + place % 2, place // 2, left // 2
    return total % 2


def edge_kernel(
    from_outer, from_mate, to_mate, to_outer, m_ref, w1, w2a, g1_in, g2_in, x3_own, e3_own, s3_own, y_own, z_own,
    kept_ref, sent_ref, d_ref, s_ref,
    x3_far, e3_far, s3_far, y_far, z_far, h3,
):
    metric = m_ref[...]
    c = to_mate.shape[2]
    odd = lax.axis_index("lon") % 2 == 1
    low, mid, high = slice(0, c), slice(c, 2 * c), slice(2 * c, 3 * c)
    far, own = (0, 1, 6, 7), (2, 3, 4, 5)

    def both(outside, inside):
        places = {i: (outside, k) for k, i in enumerate(far)}
        places.update({i: (inside, k) for k, i in enumerate(own)})
        return Columns(places)

    x3, e3, s3, y, z = (
        both(*pair)
        for pair in (
            (x3_far, x3_own), (e3_far, e3_own), (s3_far, s3_own), (y_far, y_own), (z_far, z_own)
        )
    )
    total1, total2 = g1_in[...], g2_in[...]
    for side in range(2):
        base = 4 * side
        for k in range(2):
            i = base + 2 * side + k
            x, e = (
                jnp.where(odd, from_outer[a, k], from_mate[a, k])
                if side
                else jnp.where(odd, from_mate[a, k], from_outer[a, k])
                for a in range(2)
            )
            put_three(x3, i, x, False)
            scaled = (metric * e.astype(F32)).astype(BF16)
            put_three(s3, i, scaled, True)
            near = k != side
            one, two = (high, low) if side else (low, high)
            y[i, one, :] = dot(w1[one, :], x3[i])
            z[i, two, :] = dot(w2a[two, :], s3[i])
            if near:
                put_three(e3, i, e, True)
                y[i, mid, :] = dot(w1[mid, :], x3[i])
                z[i, mid, :] = dot(w2a[mid, :], e3[i])
        for k in (1, 2):
            hidden, delta, scaled = middle(base + k, metric, y, z)
            d_ref[2 * side + k - 1] = delta
            s_ref[2 * side + k - 1] = scaled
            if k == 2 - side:
                put_three(h3, side, hidden, False)
                j = base + k
                total2 = total2 + dot_nt(three_rows(e3, s3, j), h3[side])
                total1 = total1 + jnp.concatenate(
                    [dot_nt(scaled, x3[j - 1]), dot_nt(delta, x3[j]), dot_nt(scaled, x3[j + 1])],
                    axis=0,
                )
    keeps_second = parity() == 1
    for ref, total in (
        (kept_ref, jnp.where(keeps_second, total2, total1)),
        (sent_ref, jnp.where(keeps_second, total1, total2)),
    ):
        half = total.shape[0] // 2
        tail = total[:, 2 * c :]
        ref[0 : 2 * half, :] = total[:, 0 : 2 * c].astype(ref.dtype)
        ref[2 * half :, :] = jnp.concatenate([tail[0:half], tail[half:]], axis=1).astype(ref.dtype)


def field_kernel(d_in, s_in, de_ref, se_ref, w1a_ref, out_ref, d3, s3, zm, zs, *, start):
    c, n = d_in.shape[1], d_in.shape[0]
    count = out_ref.shape[0]
    sides = jnp.concatenate([w1a_ref[0:c, :], w1a_ref[2 * c :, :]], axis=0)
    edges = {-1: 0, 0: 1, n - 1: 2, n: 3}
    for place in range(count + 2):
        i = start + place - 1
        d, s = (de_ref[edges[i]], se_ref[edges[i]]) if i in edges else (d_in[i], s_in[i])
        put_three(d3, place, d, True)
        put_three(s3, place, s, True)
        zm[place] = dot(w1a_ref[c : 2 * c, :], d3[place])
        zs[place] = dot(sides, s3[place])
        if place >= 2:
            out_ref[place - 2] = zm[place - 1] + (zs[place, 0:c, :] + zs[place - 2, c:, :])


def assemble_kernel(*refs):
    e_ref, parts, out_ref, ef = refs[0], refs[1:-2], refs[-2], refs[-1]
    c, n, lat = out_ref.shape
    i = 0
    for part in parts:
        for k in range(part.shape[0]):
            grad = part[k]
            for t, at in strided(ef, i, c, n):
                ef[at, :] = e_ref[at, :] + grad[:, t * 128 : (t + 1) * 128]
            i += 1
    for k in range(lat // 128):
        part = ef[k * c * n : (k + 1) * c * n, :].reshape(c, n, 128)
        out_ref[:, :, k * 128 : (k + 1) * 128] = part.astype(BF16)


def final_kernel(mine_ref, theirs_ref, out1_ref, out2_ref):
    c = out1_ref.shape[-1]
    odd = parity() == 1
    mine, theirs = mine_ref[...], theirs_ref[...]
    for out, packed in (
        (out1_ref, jnp.where(odd, theirs, mine)),
        (out2_ref, jnp.where(odd, mine, theirs)),
    ):
        tail = packed[3 * c :]
        tail = jnp.concatenate([tail[:, 0:c], tail[:, c:]], axis=0)
        for p in range(3):
            rows = slice(p * c, (p + 1) * c)
            out[p, 0] = packed[rows, 0:c]
            out[p, 1] = packed[rows, c:]
            out[p, 2] = tail[rows]


def vmem(count):
    return [pl.BlockSpec(memory_space=pltpu.VMEM)] * count


def size_of(shapes):
    return sum(math.prod(s) * jnp.dtype(d).itemsize for s, d in shapes)


def call(kernel, outs, scratch, *args, specs=None):
    mib = 2**20
    buffers = [s for s in scratch if isinstance(s, tuple)]
    limit = size_of(buffers) + size_of(outs) + size_of([(a.shape, a.dtype) for a in args])
    return pl.pallas_call(
        kernel,
        out_shape=[jax.ShapeDtypeStruct(s, d) for s, d in outs],
        in_specs=specs or vmem(len(args)),
        out_specs=vmem(len(outs)),
        scratch_shapes=[pltpu.VMEM(*s) if isinstance(s, tuple) else s for s in scratch],
        compiler_params=pltpu.CompilerParams(vmem_limit_bytes=(limit // mib + 6) * mib),
    )(*args)


def exchange(value, pairs):
    return lax.ppermute(value, ("dp", "lon"), pairs)


def one_sample(x, e, kernel_first, kernel_second, metric):
    c, n, lat = x.shape
    wide = 3 * c
    chunks = 1
    count = lax.axis_size("dp") * lax.axis_size("lon")
    lon = lax.axis_size("lon")
    mates = [(i, i ^ 1) for i in range(count)]
    outers = [
        (i, i // lon * lon + (i % lon + (1 if i % lon % 2 else -1)) % lon) for i in range(count)
    ]
    strided_form = ((c * n * lat // 128, 128), F32)
    column = (wide, lat)
    halo = ((2, 2, c, lat), BF16)
    square = (wide, wide)
    inputs = (x, e, metric, kernel_first, kernel_second)
    xf, ef, to_mate, to_outer, row, w1, w1a, w2a = call(
        pack_kernel,
        [strided_form] * 2 + [halo] * 2 + [((1, lat), F32)] + [(square, BF16)] * 3,
        [((c, n, lat), BF16)] * 2
        + [((lat,), F32)]
        + [((3, 3, c, c), BF16)] * 2
        + [pltpu.SemaphoreType.DMA((2, chunks)), pltpu.SemaphoreType.DMA((3,))],
        *(pltpu.with_memory_space_constraint(a, pltpu.HBM) for a in inputs),
        specs=[pl.BlockSpec(memory_space=pltpu.HBM)] * len(inputs),
    )
    from_outer = exchange(to_outer, outers)
    from_mate = exchange(to_mate, mates)
    four = [((4,) + column, BF16)] * 3 + [((4,) + column, F32)] * 2
    g1, g2, d, s, *own = call(
        interior_kernel,
        [(square, F32)] * 2 + [((n, c, lat), BF16)] * 2 + four,
        [((n,) + column, BF16)] * 3 + [((n,) + column, F32)] * 2 + [((n,) + column, BF16)],
        xf, ef, w1, w2a, row,
    )
    packed = (3 * wide // 2, 2 * c)
    kept, sent, de, se = call(
        edge_kernel,
        [(packed, F32), (packed, BF16)] + [((4, c, lat), BF16)] * 2,
        four + [((2,) + column, BF16)],
        from_outer, from_mate, to_mate, to_outer, row, w1, w2a, g1, g2, *own,
    )
    return kept, sent, (d, s, de, se, w1a), ef


def field_parts(parts, pieces):
    n, c, lat = parts[0].shape
    wide = 3 * c
    made, start = [], 0
    for k in range(pieces):
        stop = n * (k + 1) // pieces
        count = stop - start
        made.append(
            functools.partial(
                call,
                functools.partial(field_kernel, start=start),
                [((count, c, lat), F32)],
                [((count + 2, wide, lat), BF16)] * 2
                + [((count + 2, c, lat), F32), ((count + 2, 2 * c, lat), F32)],
                *parts,
            )
        )
        start = stop
    return made


def assemble(e, grads):
    n = sum(g.shape[0] for g in grads)
    _, c, lat = grads[0].shape
    return call(
        assemble_kernel, [((c, n, lat), BF16)], [((c * n * lat // 128, 128), F32)], e, *grads
    )[0]


def sum_everywhere(kept, sent, factor, jobs):
    dp, lon = lax.axis_size("dp"), lax.axis_size("lon")
    count = dp * lon
    swap = [(i, i ^ 1) for i in range(count)]
    results = []

    def beside(sent, got):
        if jobs:
            job, arguments = jobs.pop(0)
            sent, arguments = lax.optimization_barrier((sent, arguments(results)))
            results.append(job(*arguments))
            got, results[-1] = lax.optimization_barrier((got, results[-1]))
        return sent, got

    _, got = beside(sent, exchange(sent, swap))
    total = kept + got.astype(F32)
    along_lon = [1 << k for k in range(1, lon.bit_length() - 1)]
    along_dp = [lon << k for k in range(dp.bit_length() - 1)]
    bits = []
    while along_lon or along_dp:
        if along_dp:
            bits.append(along_dp.pop(0))
        if along_lon:
            bits.append(along_lon.pop())
    other = list(bits)
    for k in range(0, len(bits) - 1, 2):
        other[k], other[k + 1] = bits[k + 1], bits[k]
    for even_bit, odd_bit in zip(bits, other):
        sent = total.astype(BF16)
        got = exchange(
            sent, [(i, i ^ 1 ^ (odd_bit if i.bit_count() & 1 else even_bit)) for i in range(count)]
        )
        sent, got = beside(sent, got)
        total = sent.astype(F32) + got.astype(F32)
    for job in jobs:
        results.append(job[0](*job[1](results)))
    mine = (total * factor).astype(BF16)
    return mine, exchange(mine, swap), results


def per_device(fields, cotangent, kernel_first, kernel_second, metric):
    samples, c, n, lat = fields.shape
    counted = (
        float(samples * lax.axis_size("dp")) * float(n * lax.axis_size("lon")) * float(lat)
    )
    factor = jnp.float32(1.0 / counted**0.5)
    kept = sent = None
    jobs = []
    pieces = 2
    for b in range(samples):
        k, t, parts, ef = one_sample(fields[b], cotangent[b], kernel_first, kernel_second, metric)
        kept = k if kept is None else kept + k
        sent = t if sent is None else (sent.astype(F32) + t.astype(F32)).astype(BF16)
        for job in field_parts(parts, pieces):
            jobs.append((lambda *args, job=job: job.func(*job.args[:3], *args)[0], lambda done, job=job: job.args[3:]))
        jobs.append((
            lambda *args: assemble(args[0], args[1:]),
            lambda done, ef=ef: (ef,) + tuple(done[-pieces:]),
        ))
    mine, theirs, results = sum_everywhere(kept, sent, factor, jobs)
    field_grad = jnp.stack(results[pieces :: pieces + 1])
    grad_first, grad_second = call(
        final_kernel, [((3, 3, c, c), BF16)] * 2, [], mine, theirs
    )
    return field_grad, grad_first, grad_second


def solution(mesh):
    placed = (P("dp", None, "lon", None), P("dp", None, "lon", None), P(), P(), P())
    return jax.shard_map(
        per_device,
        mesh=mesh,
        in_specs=placed,
        out_specs=(P("dp", None, "lon", None), P(), P()),
        check_vma=False,
    )
```

```python
import functools
import math

import jax
import jax.numpy as jnp
from jax import lax
from jax.experimental import pallas as pl
from jax.experimental.pallas import tpu as pltpu
from jax.sharding import PartitionSpec as P

gelu_coef = 0.7978845608
F32 = jnp.float32
BF16 = jnp.bfloat16
NT = (((1,), (1,)), ((), ()))


def gelu_pair(u):
    square = u * u
    inner = jnp.tanh(u * (gelu_coef + (gelu_coef * 0.044715) * square))
    a = 0.5 + 0.5 * inner
    value = u * a
    twice = 2.0 * gelu_coef + (6.0 * gelu_coef * 0.044715) * square
    return value, a + (value - value * a) * twice


def neighbours(v):
    lanes = 128
    tiles = [v[:, k : k + lanes] for k in range(0, v.shape[-1], lanes)]
    lane = lax.broadcasted_iota(jnp.int32, tiles[0].shape, 1)
    zero = jnp.zeros_like(tiles[0])
    up = [zero] + [pltpu.roll(t, 1, 1) for t in tiles]
    down = [pltpu.roll(t, lanes - 1, 1) for t in tiles] + [zero]
    below = [jnp.where(lane == 0, up[k], up[k + 1]) for k in range(len(tiles))]
    above = [jnp.where(lane == lanes - 1, down[k + 1], down[k]) for k in range(len(tiles))]
    return jnp.concatenate(below, axis=1), jnp.concatenate(above, axis=1)


def dot(a, b):
    return jnp.dot(a, b, preferred_element_type=F32)


def dot_nt(a, b):
    return lax.dot_general(a, b, NT, preferred_element_type=F32)


def three(v, adjoint):
    below, above = neighbours(v)
    return jnp.concatenate([above, v, below] if adjoint else [below, v, above], axis=0)


def prepare(k_ref, forward_ref, adjoint_ref):
    c = k_ref.shape[-1]
    for p in range(3):
        if forward_ref is not None:
            forward_ref[p * c : (p + 1) * c, :] = jnp.concatenate(
                [k_ref[p, q].astype(F32) for q in range(3)], axis=1
            ).astype(BF16)
        adjoint_ref[p * c : (p + 1) * c, :] = jnp.concatenate(
            [k_ref[p, q].astype(F32).T for q in range(3)], axis=1
        ).astype(BF16)


def products(i, w1, w2a, x3, e3, s3, y, z):
    c = w1.shape[0] // 3
    y[i] = dot(w1[...], x3)
    z[i, c : 2 * c, :] = dot(w2a[c : 2 * c, :], e3)
    sides = dot(jnp.concatenate([w2a[0:c, :], w2a[2 * c :, :]], axis=0), s3)
    z[i, 0:c, :] = sides[0:c]
    z[i, 2 * c :, :] = sides[c:]


def middle(u, grad, metric):
    hidden, slope = gelu_pair(u)
    delta = (grad * slope).astype(BF16)
    return hidden.astype(BF16), delta, (metric * delta.astype(F32)).astype(BF16)


def edges_term(
    t, fields, upstream, upstream_scaled, near_fields, near_scaled, delta, delta_scaled, hidden
):
    first = t == 0
    rows = []
    for p in range(3):
        left, right = [], []
        for side, (own, inner) in enumerate(((0, 1), (3, 2))):
            if p == 1:
                one, two, three_fields = delta[side], upstream[side], fields[own]
            else:
                one = delta_scaled[side]
                if (p == 0) == (side == 0):
                    two, three_fields = upstream_scaled[side], near_fields[side]
                else:
                    two, three_fields = near_scaled[side], fields[inner]
            left.append(jnp.where(first, one, two))
            right.append(jnp.where(first, three_fields, hidden[side]))
        rows.append(dot_nt(jnp.concatenate(left, axis=1), jnp.concatenate(right, axis=1)))
    return jnp.concatenate(rows, axis=0)


def put_packed(ref, total):
    half = total.shape[0] // 2
    wide = total.shape[1] // 3 * 2
    tail = total[:, wide:]
    ref[0 : 2 * half, :] = total[:, 0:wide].astype(ref.dtype)
    ref[2 * half :, :] = jnp.concatenate([tail[0:half], tail[half:]], axis=1).astype(ref.dtype)


def scatter_out(ref, value, first=0):
    c, n, lat = value.shape
    value = value.astype(F32).reshape(c * n, lat)
    whole = ref.shape[0] * 128 // lat
    for k in range(lat // 128):
        at = k * whole + first
        ref[at : at + c * n, :] = value[:, k * 128 : (k + 1) * 128]


def strided(ref, i, c, n):
    count = ref.shape[0] // (c * n)
    return [(k, pl.ds(k * c * n + i, c, stride=n)) for k in range(count)]


def column(ref, i, c, n):
    return jnp.concatenate([ref[at, :] for _, at in strided(ref, i, c, n)], axis=1)


def pack_kernel(
    x_hbm, e_hbm, m_hbm, k1_hbm, k2_hbm,
    xf, ef, mate_ref, outer_ref, row_ref, w1_ref, w1a_ref, w2a_ref,
    xs, es, ms, k1s, k2s, sems, small_sems,
):
    c, n, lat = x_hbm.shape
    chunks = sems.shape[1]
    w = c // chunks
    small = [
        pltpu.make_async_copy(src, dst, small_sems.at[k])
        for k, (src, dst) in enumerate(((k1_hbm, k1s), (k2_hbm, k2s), (m_hbm, ms)))
    ]
    for copy in small:
        copy.start()
    copies = []
    for k in range(chunks):
        for a, (src, dst) in enumerate(((x_hbm, xs), (e_hbm, es))):
            rows = pl.ds(k * w, w)
            copies.append(pltpu.make_async_copy(src.at[rows], dst.at[rows], sems.at[a, k]))
            copies[-1].start()
    for copy in small:
        copy.wait()
    row_ref[...] = ms[...].reshape(1, lat)
    prepare(k1s, w1_ref, w1a_ref)
    prepare(k2s, None, w2a_ref)
    for k in range(chunks):
        for a, (src, dst) in enumerate(((xs, xf), (es, ef))):
            copies[2 * k + a].wait()
            scatter_out(dst, src[k * w : (k + 1) * w], k * w * n)
    odd = lax.axis_index("lon") % 2 == 1
    for a, source in enumerate((xf, ef)):
        for k in range(2):
            low = column(source, k, c, n).astype(BF16)
            high = column(source, n - 2 + k, c, n).astype(BF16)
            mate_ref[a, k] = jnp.where(odd, low, high)
            outer_ref[a, k] = jnp.where(odd, high, low)


def interior_kernel(
    xf, ef, w1_ref, w2a_ref, m_ref,
    g1_ref, g2_ref, d_ref, s_ref, fields, upstream, upstream_scaled, u_ref, grad_ref, y_ref, z_ref,
    x3, e, es, y, z, h3,
):
    n, c, lat = d_ref.shape
    low, mid, high = slice(0, c), slice(c, 2 * c), slice(2 * c, 3 * c)
    metric = m_ref[...]
    blank = jnp.zeros((c, lat), BF16)
    for i in (0, n - 1):
        d_ref[i] = blank
        s_ref[i] = blank
    g1_ref[...] = jnp.zeros_like(g1_ref)
    g2_ref[...] = jnp.zeros_like(g2_ref)

    def terms(plain, scaled, value, columns):
        left = [jnp.concatenate([scaled[j + 1], plain[j], scaled[j - 1]], axis=0) for j in columns]
        return dot_nt(
            jnp.concatenate(left, axis=1), jnp.concatenate([value[j] for j in columns], axis=1)
        )

    inner = list(range(1, n - 1))
    groups = [inner[k : k + 7] for k in range(0, n - 2, 7)]
    second_todo, first_todo = list(groups), list(groups)
    for i in range(n + 1):
        if i < n:
            x3[i] = three(column(xf, i, c, n).astype(BF16), False)
            wide = column(ef, i, c, n)
            e[i] = wide.astype(BF16)
            es[i] = (metric * wide).astype(BF16)
            products(i, w1_ref, w2a_ref, x3[i], three(e[i], True), three(es[i], True), y, z)
        k = i - 1
        if 0 < k < n - 1:
            u = y[k, mid, :] + metric * (y[k - 1, low, :] + y[k + 1, high, :])
            grad = z[k, mid, :] + (z[k + 1, low, :] + z[k - 1, high, :])
            hidden, delta, scaled = middle(u, grad, metric)
            h3[k] = three(hidden, False)
            d_ref[k] = delta
            s_ref[k] = scaled
        if i == 3:
            g1_ref[0:c, :] += dot_nt(s_ref[1], x3[0])
        ready = i - 2 if i < n else n - 2
        if second_todo and second_todo[0][-1] <= ready:
            g2_ref[...] += terms(e, es, h3, second_todo.pop(0))
        if first_todo and first_todo[0][-1] <= (ready - 1 if i < n else ready):
            g1_ref[...] += terms(d_ref, s_ref, x3, first_todo.pop(0))
    g1_ref[2 * c :, :] += dot_nt(s_ref[n - 2], x3[n - 1])
    for side, own, next_in, one, two in ((0, 0, 1, low, high), (1, n - 1, n - 2, high, low)):
        u_ref[side] = y[own, mid, :] + metric * y[next_in, two, :]
        grad_ref[side] = z[own, mid, :] + z[next_in, one, :]
        y_ref[side] = y[own, two, :]
        z_ref[side] = z[own, one, :]
        upstream[side] = e[own]
        upstream_scaled[side] = es[next_in]
    for k, i in enumerate((0, 1, n - 2, n - 1)):
        fields[k] = x3[i]


def parity():
    place = lax.axis_index("dp") * lax.axis_size("lon") + lax.axis_index("lon")
    total, left = 0, lax.axis_size("dp") * lax.axis_size("lon") - 1
    while left:
        total, place, left = total + place % 2, place // 2, left // 2
    return total % 2


def beyond(odd, from_mate, from_outer, side, array, distance):
    k = distance - 1 if side else 2 - distance
    low_is_mate = jnp.where(odd, from_mate[array, k], from_outer[array, k])
    high_is_mate = jnp.where(odd, from_outer[array, k], from_mate[array, k])
    return high_is_mate if side else low_is_mate


def edge_kernel(
    from_outer, from_mate, m_ref, w1, w2a, g1, g2, fields, upstream, upstream_scaled, u_ref, grad_ref,
    sent_ref, near_fields, near_scaled, delta, delta_scaled, hidden,
):
    metric = m_ref[...]
    c = from_mate.shape[2]
    low, high = slice(0, c), slice(2 * c, 3 * c)
    odd = lax.axis_index("lon") % 2 == 1
    t = 1 - parity()
    for side, one, two in ((0, low, high), (1, high, low)):
        x, e = (beyond(odd, from_mate, from_outer, side, a, 1) for a in range(2))
        near_fields[side] = three(x, False)
        near_scaled[side] = (metric * e.astype(F32)).astype(BF16)
        u = u_ref[side] + metric * dot(w1[one, :], near_fields[side])
        grad = grad_ref[side] + dot(w2a[two, :], three(near_scaled[side], True))
        h, delta[side], delta_scaled[side] = middle(u, grad, metric)
        hidden[side] = three(h, False)
    total = edges_term(
        t, fields, upstream, upstream_scaled, near_fields, near_scaled, delta, delta_scaled, hidden
    )
    put_packed(sent_ref, total + jnp.where(t == 0, g1[...], g2[...]))


def kept_kernel(
    from_outer, from_mate, m_ref, w1, w2a, g1, g2, fields, upstream, upstream_scaled, y_ref, z_ref,
    near_fields, near_scaled, delta, delta_scaled, hidden,
    kept_ref, near_delta, near_delta_scaled,
):
    metric = m_ref[...]
    c = from_mate.shape[2]
    low, mid, high = slice(0, c), slice(c, 2 * c), slice(2 * c, 3 * c)
    odd = lax.axis_index("lon") % 2 == 1
    t = parity()
    total = edges_term(
        t, fields, upstream, upstream_scaled, near_fields, near_scaled, delta, delta_scaled, hidden
    )
    put_packed(kept_ref, total + jnp.where(t == 0, g1[...], g2[...]))
    for side, one, two in ((0, low, high), (1, high, low)):
        x, e = (beyond(odd, from_mate, from_outer, side, a, 2) for a in range(2))
        near_e = beyond(odd, from_mate, from_outer, side, 1, 1)
        scaled = (metric * e.astype(F32)).astype(BF16)
        u = dot(w1[mid, :], near_fields[side]) + metric * (
            dot(w1[one, :], three(x, False)) + y_ref[side]
        )
        grad = dot(w2a[mid, :], three(near_e, True)) + (
            dot(w2a[two, :], three(scaled, True)) + z_ref[side]
        )
        _, near_delta[side], near_delta_scaled[side] = middle(u, grad, metric)


def field_kernel(
    d_in, s_in, delta, delta_scaled, near_delta, near_delta_scaled, w1a_ref, out_ref, zm, zs, *, start
):
    c, n = d_in.shape[1], d_in.shape[0]
    count = out_ref.shape[0]
    sides = jnp.concatenate([w1a_ref[0:c, :], w1a_ref[2 * c :, :]], axis=0)
    edges = {
        -1: (near_delta, near_delta_scaled, 0),
        0: (delta, delta_scaled, 0),
        n - 1: (delta, delta_scaled, 1),
        n: (near_delta, near_delta_scaled, 1),
    }
    for place in range(count + 2):
        i = start + place - 1
        plain, scaled, k = edges.get(i, (d_in, s_in, i))
        if 0 < place < count + 1:
            zm[place] = dot(w1a_ref[c : 2 * c, :], three(plain[k], True))
        zs[place] = dot(sides, three(scaled[k], True))
        if place >= 2:
            out_ref[place - 2] = zm[place - 1] + (zs[place, 0:c, :] + zs[place - 2, c:, :])


def assemble_kernel(*refs):
    e_ref, parts, out_ref, ef = refs[0], refs[1:-2], refs[-2], refs[-1]
    c, n, lat = out_ref.shape
    i = 0
    for part in parts:
        for k in range(part.shape[0]):
            grad = part[k]
            for t, at in strided(ef, i, c, n):
                ef[at, :] = e_ref[at, :] + grad[:, t * 128 : (t + 1) * 128]
            i += 1
    for k in range(lat // 128):
        part = ef[k * c * n : (k + 1) * c * n, :].reshape(c, n, 128)
        out_ref[:, :, k * 128 : (k + 1) * 128] = part.astype(BF16)


def final_kernel(mine_ref, theirs_ref, out1_ref, out2_ref):
    c = out1_ref.shape[-1]
    odd = parity() == 1
    mine, theirs = mine_ref[...], theirs_ref[...]
    for out, packed in (
        (out1_ref, jnp.where(odd, theirs, mine)),
        (out2_ref, jnp.where(odd, mine, theirs)),
    ):
        tail = packed[3 * c :]
        tail = jnp.concatenate([tail[:, 0:c], tail[:, c:]], axis=0)
        for p in range(3):
            rows = slice(p * c, (p + 1) * c)
            out[p, 0] = packed[rows, 0:c]
            out[p, 1] = packed[rows, c:]
            out[p, 2] = tail[rows]


def vmem(count):
    return [pl.BlockSpec(memory_space=pltpu.VMEM)] * count


def size_of(shapes):
    return sum(math.prod(s) * jnp.dtype(d).itemsize for s, d in shapes)


def call(kernel, outs, scratch, *args, specs=None):
    mib = 2**20
    buffers = [s for s in scratch if isinstance(s, tuple)]
    limit = size_of(buffers) + size_of(outs) + size_of([(a.shape, a.dtype) for a in args])
    return pl.pallas_call(
        kernel,
        out_shape=[jax.ShapeDtypeStruct(s, d) for s, d in outs],
        in_specs=specs or vmem(len(args)),
        out_specs=vmem(len(outs)),
        scratch_shapes=[pltpu.VMEM(*s) if isinstance(s, tuple) else s for s in scratch],
        compiler_params=pltpu.CompilerParams(vmem_limit_bytes=(limit // mib + 6) * mib),
    )(*args)


def exchange(value, pairs):
    return lax.ppermute(value, ("dp", "lon"), pairs)


def one_sample(x, e, kernel_first, kernel_second, metric):
    c, n, lat = x.shape
    wide = 3 * c
    chunks = 1
    count = lax.axis_size("dp") * lax.axis_size("lon")
    lon = lax.axis_size("lon")
    mates = [(i, i ^ 1) for i in range(count)]
    outers = [
        (i, i // lon * lon + (i % lon + (1 if i % lon % 2 else -1)) % lon) for i in range(count)
    ]
    strided_form = ((c * n * lat // 128, 128), F32)
    column = (wide, lat)
    halo = ((2, 2, c, lat), BF16)
    square = (wide, wide)
    inputs = (x, e, metric, kernel_first, kernel_second)
    xf, ef, to_mate, to_outer, row, w1, w1a, w2a = call(
        pack_kernel,
        [strided_form] * 2 + [halo] * 2 + [((1, lat), F32)] + [(square, BF16)] * 3,
        [((c, n, lat), BF16)] * 2
        + [((lat,), F32)]
        + [((3, 3, c, c), BF16)] * 2
        + [pltpu.SemaphoreType.DMA((2, chunks)), pltpu.SemaphoreType.DMA((3,))],
        *(pltpu.with_memory_space_constraint(a, pltpu.HBM) for a in inputs),
        specs=[pl.BlockSpec(memory_space=pltpu.HBM)] * len(inputs),
    )
    from_outer = exchange(to_outer, outers)
    from_mate = exchange(to_mate, mates)
    wide_columns = ((n,) + column, F32)
    pair = ((2, c, lat), F32)
    two = ((2, c, lat), BF16)
    two_wide = ((2,) + column, BF16)
    g1, g2, d, s, fields, upstream, upstream_scaled, u, grad, y, z = call(
        interior_kernel,
        [(square, F32)] * 2
        + [((n, c, lat), BF16)] * 2
        + [((4,) + column, BF16)]
        + [two] * 2
        + [pair] * 4,
        [((n,) + column, BF16)]
        + [((n, c, lat), BF16)] * 2
        + [wide_columns] * 2
        + [((n,) + column, BF16)],
        xf, ef, w1, w2a, row,
    )
    packed = (3 * wide // 2, 2 * c)
    common = (from_outer, from_mate, row, w1, w2a, g1, g2, fields, upstream, upstream_scaled)
    sent, *edge = call(
        edge_kernel, [(packed, BF16), two_wide, two, two, two, two_wide], [], *common, u, grad
    )
    near_fields, near_scaled, delta, delta_scaled, hidden = edge

    def keep(done, gate):
        return call(
            kept_kernel, [(packed, F32), two, two], [],
            *common, y, z, near_fields, near_scaled, delta, delta_scaled, gate(hidden),
        )

    def part(done, gate, start, count):
        return call(
            functools.partial(field_kernel, start=start),
            [((count, c, lat), F32)],
            [((count + 2, c, lat), F32), ((count + 2, 2 * c, lat), F32)],
            d, s, delta, delta_scaled, done[0][1], done[0][2], gate(w1a),
        )

    def assemble(done, gate):
        return call(
            assemble_kernel, [((c, n, lat), BF16)], [strided_form],
            ef, done[1][0], gate(done[2][0]),
        )

    half = n // 2
    return sent, [
        keep,
        lambda done, gate: part(done, gate, 0, half),
        lambda done, gate: part(done, gate, half, n - half),
        assemble,
    ]


def sum_everywhere(sent, jobs, factor):
    dp, lon = lax.axis_size("dp"), lax.axis_size("lon")
    count = dp * lon
    swap = [(i, i ^ 1) for i in range(count)]
    jobs, done = list(jobs), []

    def beside(sent, pairs):
        got = exchange(sent, pairs)
        if jobs:
            result = jobs.pop(0)(done, lambda x: lax.optimization_barrier((sent, x))[1])
            got, first = lax.optimization_barrier((got, result[0]))
            done.append([first] + list(result[1:]))
        return got

    got = beside(sent, swap)
    total = done[0][0] + got.astype(F32)
    along_lon = [1 << k for k in range(1, lon.bit_length() - 1)]
    along_dp = [lon << k for k in range(dp.bit_length() - 1)]
    bits = []
    while along_lon or along_dp:
        if along_dp:
            bits.append(along_dp.pop(0))
        if along_lon:
            bits.append(along_lon.pop())
    other = list(bits)
    for k in range(0, len(bits) - 1, 2):
        other[k], other[k + 1] = bits[k + 1], bits[k]
    for even_bit, odd_bit in zip(bits, other):
        sent = total.astype(BF16)
        got = beside(
            sent, [(i, i ^ 1 ^ (odd_bit if i.bit_count() & 1 else even_bit)) for i in range(count)]
        )
        total = sent.astype(F32) + got.astype(F32)
    while jobs:
        done.append(jobs.pop(0)(done, lambda x: x))
    mine = (total * factor).astype(BF16)
    return mine, exchange(mine, swap), done


def per_device(fields, cotangent, kernel_first, kernel_second, metric):
    samples, c, n, lat = fields.shape
    counted = (
        float(samples * lax.axis_size("dp")) * float(n * lax.axis_size("lon")) * float(lat)
    )
    factor = jnp.float32(1.0 / counted**0.5)
    sent, jobs = one_sample(fields[0], cotangent[0], kernel_first, kernel_second, metric)
    mine, theirs, done = sum_everywhere(sent, jobs, factor)
    grad_first, grad_second = call(
        final_kernel, [((3, 3, c, c), BF16)] * 2, [], mine, theirs
    )
    return done[-1][0][None], grad_first, grad_second


def solution(mesh):
    placed = (P("dp", None, "lon", None), P("dp", None, "lon", None), P(), P(), P())
    return jax.shard_map(
        per_device,
        mesh=mesh,
        in_specs=placed,
        out_specs=(P("dp", None, "lon", None), P(), P()),
        check_vma=False,
    )
```

```python
import functools
import math

import jax
import jax.numpy as jnp
from jax import lax
from jax.experimental import pallas as pl
from jax.experimental.pallas import tpu as pltpu
from jax.sharding import PartitionSpec as P

gelu_coef = 0.7978845608
F32 = jnp.float32
BF16 = jnp.bfloat16
NT = (((1,), (1,)), ((), ()))


def gelu_pair(u):
    square = u * u
    inner = jnp.tanh(u * (gelu_coef + (gelu_coef * 0.044715) * square))
    a = 0.5 + 0.5 * inner
    value = u * a
    twice = 2.0 * gelu_coef + (6.0 * gelu_coef * 0.044715) * square
    return value, a + (value - value * a) * twice


def neighbours(v):
    lanes = 128
    tiles = [v[:, k : k + lanes] for k in range(0, v.shape[-1], lanes)]
    lane = lax.broadcasted_iota(jnp.int32, tiles[0].shape, 1)
    zero = jnp.zeros_like(tiles[0])
    up = [zero] + [pltpu.roll(t, 1, 1) for t in tiles]
    down = [pltpu.roll(t, lanes - 1, 1) for t in tiles] + [zero]
    below = [jnp.where(lane == 0, up[k], up[k + 1]) for k in range(len(tiles))]
    above = [jnp.where(lane == lanes - 1, down[k + 1], down[k]) for k in range(len(tiles))]
    return jnp.concatenate(below, axis=1), jnp.concatenate(above, axis=1)


def dot(a, b):
    return jnp.dot(a, b, preferred_element_type=F32)


def dot_nt(a, b):
    return lax.dot_general(a, b, NT, preferred_element_type=F32)


def three(v, adjoint):
    below, above = neighbours(v)
    return jnp.concatenate([above, v, below] if adjoint else [below, v, above], axis=0)


def prepare(k_ref, forward_ref, adjoint_ref):
    c = k_ref.shape[-1]
    for p in range(3):
        if forward_ref is not None:
            forward_ref[p * c : (p + 1) * c, :] = jnp.concatenate(
                [k_ref[p, q].astype(F32) for q in range(3)], axis=1
            ).astype(BF16)
        adjoint_ref[p * c : (p + 1) * c, :] = jnp.concatenate(
            [k_ref[p, q].astype(F32).T for q in range(3)], axis=1
        ).astype(BF16)


def products(i, w1, w2a, x3, e3, s3, y, z):
    c = w1.shape[0] // 3
    y[i] = dot(w1[...], x3)
    z[i, c : 2 * c, :] = dot(w2a[c : 2 * c, :], e3)
    sides = dot(jnp.concatenate([w2a[0:c, :], w2a[2 * c :, :]], axis=0), s3)
    z[i, 0:c, :] = sides[0:c]
    z[i, 2 * c :, :] = sides[c:]


def middle(u, grad, metric):
    hidden, slope = gelu_pair(u)
    delta = (grad * slope).astype(BF16)
    return hidden.astype(BF16), delta, (metric * delta.astype(F32)).astype(BF16)


def edges_term(
    t, fields, upstream, upstream_scaled, near_fields, near_scaled, delta, delta_scaled, hidden
):
    first = t == 0
    rows = []
    for p in range(3):
        left, right = [], []
        for side, (own, inner) in enumerate(((0, 1), (3, 2))):
            if p == 1:
                one, two, three_fields = delta[side], upstream[side], fields[own]
            else:
                one = delta_scaled[side]
                if (p == 0) == (side == 0):
                    two, three_fields = upstream_scaled[side], near_fields[side]
                else:
                    two, three_fields = near_scaled[side], fields[inner]
            left.append(jnp.where(first, one, two))
            right.append(jnp.where(first, three_fields, hidden[side]))
        rows.append(dot_nt(jnp.concatenate(left, axis=1), jnp.concatenate(right, axis=1)))
    return jnp.concatenate(rows, axis=0)


def put_packed(ref, total):
    half = total.shape[0] // 2
    wide = total.shape[1] // 3 * 2
    tail = total[:, wide:]
    ref[0 : 2 * half, :] = total[:, 0:wide].astype(ref.dtype)
    ref[2 * half :, :] = jnp.concatenate([tail[0:half], tail[half:]], axis=1).astype(ref.dtype)


def turning(n, back=False, edges=False):
    shape = (64 if edges else 16 * n, 16 * n)
    row = lax.broadcasted_iota(jnp.int32, shape, 1 if back else 0)
    source = lax.broadcasted_iota(jnp.int32, shape, 0 if back else 1)
    place = lax.shift_right_logical(row, jnp.full_like(row, 4))
    if edges:
        place = jnp.where(place < 2, place, place + n - 4)
    return jnp.where(source == (row & 15) * n + place, 1.0, 0.0).astype(BF16)


def turn_columns(turn, source, target):
    c, n, lat = source.shape
    for b in range(0, c, 16):
        turned = dot(turn, source[b : b + 16].reshape(16 * n, lat)).astype(BF16)
        for i in range(turn.shape[0] // 16):
            target[i, b : b + 16, :] = turned[16 * i : 16 * (i + 1)]


def pack_kernel(
    x_hbm, e_hbm, m_hbm, x_ref, e_ref, mate_ref, outer_ref, row_ref, edges, ms, sems
):
    n, lat = x_hbm.shape[1:]
    copies = [
        pltpu.make_async_copy(src, dst, sems.at[a])
        for a, (src, dst) in enumerate(((x_hbm, x_ref), (e_hbm, e_ref), (m_hbm, ms)))
    ]
    for copy in copies:
        copy.start()
    turn = turning(n, edges=True)
    odd = lax.axis_index("lon") % 2 == 1
    for a, source in enumerate((x_ref, e_ref)):
        copies[a].wait()
        turn_columns(turn, source, edges)
        for k in range(2):
            mate_ref[a, k] = jnp.where(odd, edges[k], edges[2 + k])
            outer_ref[a, k] = jnp.where(odd, edges[2 + k], edges[k])
    copies[2].wait()
    row_ref[...] = ms[...].reshape(1, lat)


def interior_kernel(
    x_ref, e_ref, k1_ref, k2_ref, m_ref,
    e, w1_ref, w1a_ref, w2a_ref, g1_ref, g2_ref, d_ref, s_ref, fields, upstream, upstream_scaled, u_ref, grad_ref, y_ref, z_ref,
    x, x3, es, y, z, h3,
):
    n, c, lat = d_ref.shape
    low, mid, high = slice(0, c), slice(c, 2 * c), slice(2 * c, 3 * c)
    metric = m_ref[...]
    turn = turning(n)
    turn_columns(turn, x_ref, x)
    turn_columns(turn, e_ref, e)
    prepare(k1_ref, w1_ref, w1a_ref)
    prepare(k2_ref, None, w2a_ref)
    blank = jnp.zeros((c, lat), BF16)
    for i in (0, n - 1):
        d_ref[i] = blank
        s_ref[i] = blank
    g1_ref[...] = jnp.zeros_like(g1_ref)
    g2_ref[...] = jnp.zeros_like(g2_ref)

    def terms(plain, scaled, value, columns):
        left = [jnp.concatenate([scaled[j + 1], plain[j], scaled[j - 1]], axis=0) for j in columns]
        return dot_nt(
            jnp.concatenate(left, axis=1), jnp.concatenate([value[j] for j in columns], axis=1)
        )

    inner = list(range(1, n - 1))
    groups = [inner[k : k + 7] for k in range(0, n - 2, 7)]
    second_todo, first_todo = list(groups), list(groups)
    for i in range(n + 1):
        if i < n:
            x3[i] = three(x[i], False)
            es[i] = (metric * e[i].astype(F32)).astype(BF16)
            products(i, w1_ref, w2a_ref, x3[i], three(e[i], True), three(es[i], True), y, z)
        k = i - 1
        if 0 < k < n - 1:
            u = y[k, mid, :] + metric * (y[k - 1, low, :] + y[k + 1, high, :])
            grad = z[k, mid, :] + (z[k + 1, low, :] + z[k - 1, high, :])
            hidden, delta, scaled = middle(u, grad, metric)
            h3[k] = three(hidden, False)
            d_ref[k] = delta
            s_ref[k] = scaled
        if i == 3:
            g1_ref[0:c, :] += dot_nt(s_ref[1], x3[0])
        ready = i - 2 if i < n else n - 2
        if second_todo and second_todo[0][-1] <= ready:
            g2_ref[...] += terms(e, es, h3, second_todo.pop(0))
        if first_todo and first_todo[0][-1] <= (ready - 1 if i < n else ready):
            g1_ref[...] += terms(d_ref, s_ref, x3, first_todo.pop(0))
    g1_ref[2 * c :, :] += dot_nt(s_ref[n - 2], x3[n - 1])
    for side, own, next_in, one, two in ((0, 0, 1, low, high), (1, n - 1, n - 2, high, low)):
        u_ref[side] = y[own, mid, :] + metric * y[next_in, two, :]
        grad_ref[side] = z[own, mid, :] + z[next_in, one, :]
        y_ref[side] = y[own, two, :]
        z_ref[side] = z[own, one, :]
        upstream[side] = e[own]
        upstream_scaled[side] = es[next_in]
    for k, i in enumerate((0, 1, n - 2, n - 1)):
        fields[k] = x3[i]


def parity():
    place = lax.axis_index("dp") * lax.axis_size("lon") + lax.axis_index("lon")
    total, left = 0, lax.axis_size("dp") * lax.axis_size("lon") - 1
    while left:
        total, place, left = total + place % 2, place // 2, left // 2
    return total % 2


def beyond(odd, from_mate, from_outer, side, array, distance):
    k = distance - 1 if side else 2 - distance
    low_is_mate = jnp.where(odd, from_mate[array, k], from_outer[array, k])
    high_is_mate = jnp.where(odd, from_outer[array, k], from_mate[array, k])
    return high_is_mate if side else low_is_mate


def edge_kernel(
    from_outer, from_mate, m_ref, w1, w2a, g1, g2, fields, upstream, upstream_scaled, u_ref, grad_ref,
    sent_ref, near_fields, near_scaled, delta, delta_scaled, hidden,
):
    metric = m_ref[...]
    c = from_mate.shape[2]
    low, high = slice(0, c), slice(2 * c, 3 * c)
    odd = lax.axis_index("lon") % 2 == 1
    t = 1 - parity()
    for side, one, two in ((0, low, high), (1, high, low)):
        x, e = (beyond(odd, from_mate, from_outer, side, a, 1) for a in range(2))
        near_fields[side] = three(x, False)
        near_scaled[side] = (metric * e.astype(F32)).astype(BF16)
        u = u_ref[side] + metric * dot(w1[one, :], near_fields[side])
        grad = grad_ref[side] + dot(w2a[two, :], three(near_scaled[side], True))
        h, delta[side], delta_scaled[side] = middle(u, grad, metric)
        hidden[side] = three(h, False)
    total = edges_term(
        t, fields, upstream, upstream_scaled, near_fields, near_scaled, delta, delta_scaled, hidden
    )
    put_packed(sent_ref, total + jnp.where(t == 0, g1[...], g2[...]))


def kept_kernel(
    from_outer, from_mate, m_ref, w1, w2a, g1, g2, fields, upstream, upstream_scaled, y_ref, z_ref,
    near_fields, near_scaled, delta, delta_scaled, hidden,
    kept_ref, near_delta, near_delta_scaled,
):
    metric = m_ref[...]
    c = from_mate.shape[2]
    low, mid, high = slice(0, c), slice(c, 2 * c), slice(2 * c, 3 * c)
    odd = lax.axis_index("lon") % 2 == 1
    t = parity()
    total = edges_term(
        t, fields, upstream, upstream_scaled, near_fields, near_scaled, delta, delta_scaled, hidden
    )
    put_packed(kept_ref, total + jnp.where(t == 0, g1[...], g2[...]))
    for side, one, two in ((0, low, high), (1, high, low)):
        x, e = (beyond(odd, from_mate, from_outer, side, a, 2) for a in range(2))
        near_e = beyond(odd, from_mate, from_outer, side, 1, 1)
        scaled = (metric * e.astype(F32)).astype(BF16)
        u = dot(w1[mid, :], near_fields[side]) + metric * (
            dot(w1[one, :], three(x, False)) + y_ref[side]
        )
        grad = dot(w2a[mid, :], three(near_e, True)) + (
            dot(w2a[two, :], three(scaled, True)) + z_ref[side]
        )
        _, near_delta[side], near_delta_scaled[side] = middle(u, grad, metric)


def field_kernel(
    e_ref, d_in, s_in, delta, delta_scaled, near_delta, near_delta_scaled, w1a_ref, out_ref, zm, zs, *, start
):
    c, n = d_in.shape[1], d_in.shape[0]
    count = out_ref.shape[0]
    sides = jnp.concatenate([w1a_ref[0:c, :], w1a_ref[2 * c :, :]], axis=0)
    edges = {
        -1: (near_delta, near_delta_scaled, 0),
        0: (delta, delta_scaled, 0),
        n - 1: (delta, delta_scaled, 1),
        n: (near_delta, near_delta_scaled, 1),
    }
    for place in range(count + 2):
        i = start + place - 1
        plain, scaled, k = edges.get(i, (d_in, s_in, i))
        if 0 < place < count + 1:
            zm[place] = dot(w1a_ref[c : 2 * c, :], three(plain[k], True))
        zs[place] = dot(sides, three(scaled[k], True))
        if place >= 2:
            grad = zm[place - 1] + (zs[place, 0:c, :] + zs[place - 2, c:, :])
            out_ref[place - 2] = (e_ref[i - 1].astype(F32) + grad).astype(BF16)


def assemble_kernel(*refs):
    parts, out_ref = refs[:-1], refs[-1]
    c, n, lat = out_ref.shape
    turn = turning(n, back=True)
    for b in range(0, c, 16):
        rows = [part[k, b : b + 16, :] for part in parts for k in range(part.shape[0])]
        turned = dot(turn, jnp.concatenate(rows, axis=0))
        out_ref[b : b + 16] = turned.astype(BF16).reshape(16, n, lat)


def final_kernel(mine_ref, theirs_ref, out1_ref, out2_ref):
    c = out1_ref.shape[-1]
    odd = parity() == 1
    mine, theirs = mine_ref[...], theirs_ref[...]
    for out, packed in (
        (out1_ref, jnp.where(odd, theirs, mine)),
        (out2_ref, jnp.where(odd, mine, theirs)),
    ):
        tail = packed[3 * c :]
        tail = jnp.concatenate([tail[:, 0:c], tail[:, c:]], axis=0)
        for p in range(3):
            rows = slice(p * c, (p + 1) * c)
            out[p, 0] = packed[rows, 0:c]
            out[p, 1] = packed[rows, c:]
            out[p, 2] = tail[rows]


def vmem(count):
    return [pl.BlockSpec(memory_space=pltpu.VMEM)] * count


def size_of(shapes):
    return sum(math.prod(s) * jnp.dtype(d).itemsize for s, d in shapes)


def call(kernel, outs, scratch, *args, specs=None):
    mib = 2**20
    buffers = [s for s in scratch if isinstance(s, tuple)]
    limit = size_of(buffers) + size_of(outs) + size_of([(a.shape, a.dtype) for a in args])
    return pl.pallas_call(
        kernel,
        out_shape=[jax.ShapeDtypeStruct(s, d) for s, d in outs],
        in_specs=specs or vmem(len(args)),
        out_specs=vmem(len(outs)),
        scratch_shapes=[pltpu.VMEM(*s) if isinstance(s, tuple) else s for s in scratch],
        compiler_params=pltpu.CompilerParams(vmem_limit_bytes=(limit // mib + 6) * mib),
    )(*args)


def exchange(value, pairs):
    return lax.ppermute(value, ("dp", "lon"), pairs)


def one_sample(x, e, kernel_first, kernel_second, metric):
    c, n, lat = x.shape
    wide = 3 * c
    count = lax.axis_size("dp") * lax.axis_size("lon")
    lon = lax.axis_size("lon")
    mates = [(i, i ^ 1) for i in range(count)]
    outers = [
        (i, i // lon * lon + (i % lon + (1 if i % lon % 2 else -1)) % lon) for i in range(count)
    ]
    turned_form = ((n, c, lat), BF16)
    column = (wide, lat)
    halo = ((2, 2, c, lat), BF16)
    square = (wide, wide)
    inputs = (x, e, metric)
    x_here, e_here, to_mate, to_outer, row = call(
        pack_kernel,
        [((c, n, lat), BF16)] * 2 + [halo] * 2 + [((1, lat), F32)],
        [((4, c, lat), BF16), ((lat,), F32), pltpu.SemaphoreType.DMA((3,))],
        *(pltpu.with_memory_space_constraint(a, pltpu.HBM) for a in inputs),
        specs=[pl.BlockSpec(memory_space=pltpu.HBM)] * len(inputs),
    )
    from_outer = exchange(to_outer, outers)
    from_mate = exchange(to_mate, mates)
    wide_columns = ((n,) + column, F32)
    pair = ((2, c, lat), F32)
    two = ((2, c, lat), BF16)
    two_wide = ((2,) + column, BF16)
    et, w1, w1a, w2a, g1, g2, d, s, fields, upstream, upstream_scaled, u, grad, y, z = call(
        interior_kernel,
        [turned_form]
        + [(square, BF16)] * 3
        + [(square, F32)] * 2
        + [turned_form] * 2
        + [((4,) + column, BF16)]
        + [two] * 2
        + [pair] * 4,
        [turned_form, ((n,) + column, BF16), turned_form]
        + [wide_columns] * 2
        + [((n,) + column, BF16)],
        x_here, e_here, kernel_first, kernel_second, row,
    )
    packed = (3 * wide // 2, 2 * c)
    common = (from_outer, from_mate, row, w1, w2a, g1, g2, fields, upstream, upstream_scaled)
    sent, *edge = call(
        edge_kernel, [(packed, BF16), two_wide, two, two, two, two_wide], [], *common, u, grad
    )
    near_fields, near_scaled, delta, delta_scaled, hidden = edge

    def keep(done, gate):
        return call(
            kept_kernel, [(packed, F32), two, two], [],
            *common, y, z, near_fields, near_scaled, delta, delta_scaled, gate(hidden),
        )

    def part(done, gate, start, count):
        return call(
            functools.partial(field_kernel, start=start),
            [((count, c, lat), BF16)],
            [((count + 2, c, lat), F32), ((count + 2, 2 * c, lat), F32)],
            et, d, s, delta, delta_scaled, done[0][1], done[0][2], gate(w1a),
        )

    def assemble(done, gate):
        return call(
            assemble_kernel, [((c, n, lat), BF16)], [], done[1][0], gate(done[2][0])
        )

    half = n // 2
    return sent, [
        keep,
        lambda done, gate: part(done, gate, 0, half),
        lambda done, gate: part(done, gate, half, n - half),
        assemble,
    ]


def sum_everywhere(sent, jobs, factor):
    dp, lon = lax.axis_size("dp"), lax.axis_size("lon")
    count = dp * lon
    swap = [(i, i ^ 1) for i in range(count)]
    jobs, done = list(jobs), []

    def beside(sent, pairs):
        got = exchange(sent, pairs)
        if jobs:
            result = jobs.pop(0)(done, lambda x: lax.optimization_barrier((sent, x))[1])
            got, first = lax.optimization_barrier((got, result[0]))
            done.append([first] + list(result[1:]))
        return got

    got = beside(sent, swap)
    total = done[0][0] + got.astype(F32)
    along_lon = [1 << k for k in range(1, lon.bit_length() - 1)]
    along_dp = [lon << k for k in range(dp.bit_length() - 1)]
    bits = []
    while along_lon or along_dp:
        if along_dp:
            bits.append(along_dp.pop(0))
        if along_lon:
            bits.append(along_lon.pop())
    other = list(bits)
    for k in range(0, len(bits) - 1, 2):
        other[k], other[k + 1] = bits[k + 1], bits[k]
    for even_bit, odd_bit in zip(bits, other):
        sent = total.astype(BF16)
        got = beside(
            sent, [(i, i ^ 1 ^ (odd_bit if i.bit_count() & 1 else even_bit)) for i in range(count)]
        )
        total = sent.astype(F32) + got.astype(F32)
    while jobs:
        done.append(jobs.pop(0)(done, lambda x: x))
    mine = (total * factor).astype(BF16)
    return mine, exchange(mine, swap), done


def per_device(fields, cotangent, kernel_first, kernel_second, metric):
    samples, c, n, lat = fields.shape
    counted = (
        float(samples * lax.axis_size("dp")) * float(n * lax.axis_size("lon")) * float(lat)
    )
    factor = jnp.float32(1.0 / counted**0.5)
    sent, jobs = one_sample(fields[0], cotangent[0], kernel_first, kernel_second, metric)
    mine, theirs, done = sum_everywhere(sent, jobs, factor)
    grad_first, grad_second = call(
        final_kernel, [((3, 3, c, c), BF16)] * 2, [], mine, theirs
    )
    return done[-1][0][None], grad_first, grad_second


def solution(mesh):
    placed = (P("dp", None, "lon", None), P("dp", None, "lon", None), P(), P(), P())
    return jax.shard_map(
        per_device,
        mesh=mesh,
        in_specs=placed,
        out_specs=(P("dp", None, "lon", None), P(), P()),
        check_vma=False,
    )
```

```python
import functools
import math

import jax
import jax.numpy as jnp
from jax import lax
from jax.experimental import pallas as pl
from jax.experimental.pallas import tpu as pltpu
from jax.sharding import PartitionSpec as P

gelu_coef = 0.7978845608
F32 = jnp.float32
BF16 = jnp.bfloat16
NT = (((1,), (1,)), ((), ()))


def gelu_pair(u):
    square = u * u
    inner = jnp.tanh(u * (gelu_coef + (gelu_coef * 0.044715) * square))
    a = 0.5 + 0.5 * inner
    value = u * a
    twice = 2.0 * gelu_coef + (6.0 * gelu_coef * 0.044715) * square
    return value, a + (value - value * a) * twice


def neighbours(v):
    lanes = 128
    tiles = [v[:, k : k + lanes] for k in range(0, v.shape[-1], lanes)]
    lane = lax.broadcasted_iota(jnp.int32, tiles[0].shape, 1)
    zero = jnp.zeros_like(tiles[0])
    up = [zero] + [pltpu.roll(t, 1, 1) for t in tiles]
    down = [pltpu.roll(t, lanes - 1, 1) for t in tiles] + [zero]
    below = [jnp.where(lane == 0, up[k], up[k + 1]) for k in range(len(tiles))]
    above = [jnp.where(lane == lanes - 1, down[k + 1], down[k]) for k in range(len(tiles))]
    return jnp.concatenate(below, axis=1), jnp.concatenate(above, axis=1)


def dot(a, b):
    return jnp.dot(a, b, preferred_element_type=F32)


def dot_nt(a, b):
    return lax.dot_general(a, b, NT, preferred_element_type=F32)


def three(v, adjoint):
    below, above = neighbours(v)
    return jnp.concatenate([above, v, below] if adjoint else [below, v, above], axis=0)


def prepare(k_ref, forward_ref, adjoint_ref):
    c = k_ref.shape[-1]
    for p in range(3):
        if forward_ref is not None:
            forward_ref[p * c : (p + 1) * c, :] = jnp.concatenate(
                [k_ref[p, q].astype(F32) for q in range(3)], axis=1
            ).astype(BF16)
        adjoint_ref[p * c : (p + 1) * c, :] = jnp.concatenate(
            [k_ref[p, q].astype(F32).T for q in range(3)], axis=1
        ).astype(BF16)


def products(i, w1, w2a, x3, e3, s3, y, z):
    c = w1.shape[0] // 3
    y[i] = dot(w1[...], x3)
    z[i, c : 2 * c, :] = dot(w2a[c : 2 * c, :], e3)
    sides = dot(jnp.concatenate([w2a[0:c, :], w2a[2 * c :, :]], axis=0), s3)
    z[i, 0:c, :] = sides[0:c]
    z[i, 2 * c :, :] = sides[c:]


def middle(u, grad, metric):
    hidden, slope = gelu_pair(u)
    delta = (grad * slope).astype(BF16)
    return hidden.astype(BF16), delta, (metric * delta.astype(F32)).astype(BF16)


def edges_term(
    t, fields, upstream, upstream_scaled, near_fields, near_scaled, delta, delta_scaled, hidden
):
    first = t == 0
    rows = []
    for p in range(3):
        left, right = [], []
        for side, (own, inner) in enumerate(((0, 1), (3, 2))):
            if p == 1:
                one, two, three_fields = delta[side], upstream[side], fields[own]
            else:
                one = delta_scaled[side]
                if (p == 0) == (side == 0):
                    two, three_fields = upstream_scaled[side], near_fields[side]
                else:
                    two, three_fields = near_scaled[side], fields[inner]
            left.append(jnp.where(first, one, two))
            right.append(jnp.where(first, three_fields, hidden[side]))
        rows.append(dot_nt(jnp.concatenate(left, axis=1), jnp.concatenate(right, axis=1)))
    return jnp.concatenate(rows, axis=0)


def put_packed(ref, total):
    half = total.shape[0] // 2
    wide = total.shape[1] // 3 * 2
    tail = total[:, wide:]
    ref[0 : 2 * half, :] = total[:, 0:wide].astype(ref.dtype)
    ref[2 * half :, :] = jnp.concatenate([tail[0:half], tail[half:]], axis=1).astype(ref.dtype)


def turning(n, back=False, edges=False):
    shape = (64 if edges else 16 * n, 16 * n)
    row = lax.broadcasted_iota(jnp.int32, shape, 1 if back else 0)
    source = lax.broadcasted_iota(jnp.int32, shape, 0 if back else 1)
    place = lax.shift_right_logical(row, jnp.full_like(row, 4))
    if edges:
        place = jnp.where(place < 2, place, place + n - 4)
    return jnp.where(source == (row & 15) * n + place, 1.0, 0.0).astype(BF16)


def turn_columns(turn, source, target):
    c, n, lat = source.shape
    for b in range(0, c, 16):
        turned = dot(turn, source[b : b + 16].reshape(16 * n, lat)).astype(BF16)
        for i in range(turn.shape[0] // 16):
            target[i, b : b + 16, :] = turned[16 * i : 16 * (i + 1)]


def pack_kernel(
    x_hbm, e_hbm, m_hbm, x_ref, e_ref, mate_ref, outer_ref, row_ref, edges, ms, sems
):
    n, lat = x_hbm.shape[1:]
    copies = [
        pltpu.make_async_copy(src, dst, sems.at[a])
        for a, (src, dst) in enumerate(((x_hbm, x_ref), (e_hbm, e_ref), (m_hbm, ms)))
    ]
    for copy in copies:
        copy.start()
    turn = turning(n, edges=True)
    odd = lax.axis_index("lon") % 2 == 1
    for a, source in enumerate((x_ref, e_ref)):
        copies[a].wait()
        turn_columns(turn, source, edges)
        for k in range(2):
            mate_ref[a, k] = jnp.where(odd, edges[k], edges[2 + k])
            outer_ref[a, k] = jnp.where(odd, edges[2 + k], edges[k])
    copies[2].wait()
    row_ref[...] = ms[...].reshape(1, lat)


def interior_kernel(
    x_ref, e_ref, k1_ref, k2_ref, m_ref,
    e, w1_ref, w1a_ref, w2a_ref, g1_ref, g2_ref, d_ref, s_ref, fields, upstream, upstream_scaled, u_ref, grad_ref, y_ref, z_ref,
    x, x3, es, y, z, h3,
):
    n, c, lat = d_ref.shape
    low, mid, high = slice(0, c), slice(c, 2 * c), slice(2 * c, 3 * c)
    metric = m_ref[...]
    turn = turning(n)
    turn_columns(turn, x_ref, x)
    turn_columns(turn, e_ref, e)
    prepare(k1_ref, w1_ref, w1a_ref)
    prepare(k2_ref, None, w2a_ref)
    blank = jnp.zeros((c, lat), BF16)
    for i in (0, n - 1):
        d_ref[i] = blank
        s_ref[i] = blank
    g1_ref[...] = jnp.zeros_like(g1_ref)
    g2_ref[...] = jnp.zeros_like(g2_ref)

    def terms(plain, scaled, value, columns):
        left = [jnp.concatenate([scaled[j + 1], plain[j], scaled[j - 1]], axis=0) for j in columns]
        return dot_nt(
            jnp.concatenate(left, axis=1), jnp.concatenate([value[j] for j in columns], axis=1)
        )

    inner = list(range(1, n - 1))
    groups = [inner[k : k + 7] for k in range(0, n - 2, 7)]
    second_todo, first_todo = list(groups), list(groups)
    for i in range(n + 1):
        if i < n:
            x3[i] = three(x[i], False)
            es[i] = (metric * e[i].astype(F32)).astype(BF16)
            products(i, w1_ref, w2a_ref, x3[i], three(e[i], True), three(es[i], True), y, z)
        k = i - 1
        if 0 < k < n - 1:
            u = y[k, mid, :] + metric * (y[k - 1, low, :] + y[k + 1, high, :])
            grad = z[k, mid, :] + (z[k + 1, low, :] + z[k - 1, high, :])
            hidden, delta, scaled = middle(u, grad, metric)
            h3[k] = three(hidden, False)
            d_ref[k] = delta
            s_ref[k] = scaled
        if i == 3:
            g1_ref[0:c, :] += dot_nt(s_ref[1], x3[0])
        ready = i - 2 if i < n else n - 2
        if second_todo and second_todo[0][-1] <= ready:
            g2_ref[...] += terms(e, es, h3, second_todo.pop(0))
        if first_todo and first_todo[0][-1] <= (ready - 1 if i < n else ready):
            g1_ref[...] += terms(d_ref, s_ref, x3, first_todo.pop(0))
    g1_ref[2 * c :, :] += dot_nt(s_ref[n - 2], x3[n - 1])
    for side, own, next_in, one, two in ((0, 0, 1, low, high), (1, n - 1, n - 2, high, low)):
        u_ref[side] = y[own, mid, :] + metric * y[next_in, two, :]
        grad_ref[side] = z[own, mid, :] + z[next_in, one, :]
        y_ref[side] = y[own, two, :]
        z_ref[side] = z[own, one, :]
        upstream[side] = e[own]
        upstream_scaled[side] = es[next_in]
    for k, i in enumerate((0, 1, n - 2, n - 1)):
        fields[k] = x3[i]


def parity():
    place = lax.axis_index("dp") * lax.axis_size("lon") + lax.axis_index("lon")
    total, left = 0, lax.axis_size("dp") * lax.axis_size("lon") - 1
    while left:
        total, place, left = total + place % 2, place // 2, left // 2
    return total % 2


def beyond(odd, from_mate, from_outer, side, array, distance):
    k = distance - 1 if side else 2 - distance
    low_is_mate = jnp.where(odd, from_mate[array, k], from_outer[array, k])
    high_is_mate = jnp.where(odd, from_outer[array, k], from_mate[array, k])
    return high_is_mate if side else low_is_mate


def edge_kernel(
    from_outer, from_mate, m_ref, w1, w2a, g1, g2, fields, upstream, upstream_scaled, u_ref, grad_ref,
    sent_ref, near_fields, near_scaled, delta, delta_scaled, hidden,
):
    metric = m_ref[...]
    c = from_mate.shape[2]
    low, high = slice(0, c), slice(2 * c, 3 * c)
    odd = lax.axis_index("lon") % 2 == 1
    t = 1 - parity()
    for side, one, two in ((0, low, high), (1, high, low)):
        x, e = (beyond(odd, from_mate, from_outer, side, a, 1) for a in range(2))
        near_fields[side] = three(x, False)
        near_scaled[side] = (metric * e.astype(F32)).astype(BF16)
        u = u_ref[side] + metric * dot(w1[one, :], near_fields[side])
        grad = grad_ref[side] + dot(w2a[two, :], three(near_scaled[side], True))
        h, delta[side], delta_scaled[side] = middle(u, grad, metric)
        hidden[side] = three(h, False)
    total = edges_term(
        t, fields, upstream, upstream_scaled, near_fields, near_scaled, delta, delta_scaled, hidden
    )
    put_packed(sent_ref, total + jnp.where(t == 0, g1[...], g2[...]))


def kept_kernel(
    from_outer, from_mate, m_ref, w1, w2a, g1, g2, fields, upstream, upstream_scaled, y_ref, z_ref,
    near_fields, near_scaled, delta, delta_scaled, hidden,
    kept_ref, near_delta, near_delta_scaled,
):
    metric = m_ref[...]
    c = from_mate.shape[2]
    low, mid, high = slice(0, c), slice(c, 2 * c), slice(2 * c, 3 * c)
    odd = lax.axis_index("lon") % 2 == 1
    t = parity()
    total = edges_term(
        t, fields, upstream, upstream_scaled, near_fields, near_scaled, delta, delta_scaled, hidden
    )
    put_packed(kept_ref, total + jnp.where(t == 0, g1[...], g2[...]))
    for side, one, two in ((0, low, high), (1, high, low)):
        x, e = (beyond(odd, from_mate, from_outer, side, a, 2) for a in range(2))
        near_e = beyond(odd, from_mate, from_outer, side, 1, 1)
        scaled = (metric * e.astype(F32)).astype(BF16)
        u = dot(w1[mid, :], near_fields[side]) + metric * (
            dot(w1[one, :], three(x, False)) + y_ref[side]
        )
        grad = dot(w2a[mid, :], three(near_e, True)) + (
            dot(w2a[two, :], three(scaled, True)) + z_ref[side]
        )
        _, near_delta[side], near_delta_scaled[side] = middle(u, grad, metric)


def field_kernel(
    e_ref, d_in, s_in, delta, delta_scaled, near_delta, near_delta_scaled, w1a_ref, out_ref, zm, zs, *, start
):
    c, n = d_in.shape[1], d_in.shape[0]
    count = out_ref.shape[0]
    sides = jnp.concatenate([w1a_ref[0:c, :], w1a_ref[2 * c :, :]], axis=0)
    edges = {
        -1: (near_delta, near_delta_scaled, 0),
        0: (delta, delta_scaled, 0),
        n - 1: (delta, delta_scaled, 1),
        n: (near_delta, near_delta_scaled, 1),
    }
    for place in range(count + 2):
        i = start + place - 1
        plain, scaled, k = edges.get(i, (d_in, s_in, i))
        if 0 < place < count + 1:
            zm[place] = dot(w1a_ref[c : 2 * c, :], three(plain[k], True))
        zs[place] = dot(sides, three(scaled[k], True))
        if place >= 2:
            grad = zm[place - 1] + (zs[place, 0:c, :] + zs[place - 2, c:, :])
            out_ref[place - 2] = (e_ref[i - 1].astype(F32) + grad).astype(BF16)


def assemble_kernel(*refs):
    parts, out_ref = refs[:-1], refs[-1]
    c, n, lat = out_ref.shape
    turn = turning(n, back=True)
    for b in range(0, c, 16):
        rows = [part[k, b : b + 16, :] for part in parts for k in range(part.shape[0])]
        turned = dot(turn, jnp.concatenate(rows, axis=0))
        out_ref[b : b + 16] = turned.astype(BF16).reshape(16, n, lat)


def final_kernel(mine_ref, theirs_ref, out1_ref, out2_ref):
    c = out1_ref.shape[-1]
    odd = parity() == 1
    mine, theirs = mine_ref[...], theirs_ref[...]
    for out, packed in (
        (out1_ref, jnp.where(odd, theirs, mine)),
        (out2_ref, jnp.where(odd, mine, theirs)),
    ):
        tail = packed[3 * c :]
        tail = jnp.concatenate([tail[:, 0:c], tail[:, c:]], axis=0)
        for p in range(3):
            rows = slice(p * c, (p + 1) * c)
            out[p, 0] = packed[rows, 0:c]
            out[p, 1] = packed[rows, c:]
            out[p, 2] = tail[rows]


def vmem(count):
    return [pl.BlockSpec(memory_space=pltpu.VMEM)] * count


def size_of(shapes):
    return sum(math.prod(s) * jnp.dtype(d).itemsize for s, d in shapes)


def call(kernel, outs, scratch, *args, specs=None):
    mib = 2**20
    buffers = [s for s in scratch if isinstance(s, tuple)]
    limit = size_of(buffers) + size_of(outs) + size_of([(a.shape, a.dtype) for a in args])
    return pl.pallas_call(
        kernel,
        out_shape=[jax.ShapeDtypeStruct(s, d) for s, d in outs],
        in_specs=specs or vmem(len(args)),
        out_specs=vmem(len(outs)),
        scratch_shapes=[pltpu.VMEM(*s) if isinstance(s, tuple) else s for s in scratch],
        compiler_params=pltpu.CompilerParams(vmem_limit_bytes=(limit // mib + 6) * mib),
    )(*args)


def exchange(value, pairs):
    return lax.ppermute(value, ("dp", "lon"), pairs)


def one_sample(x, e, kernel_first, kernel_second, metric):
    c, n, lat = x.shape
    wide = 3 * c
    count = lax.axis_size("dp") * lax.axis_size("lon")
    lon = lax.axis_size("lon")
    mates = [(i, i ^ 1) for i in range(count)]
    outers = [
        (i, i // lon * lon + (i % lon + (1 if i % lon % 2 else -1)) % lon) for i in range(count)
    ]
    turned_form = ((n, c, lat), BF16)
    column = (wide, lat)
    halo = ((2, 2, c, lat), BF16)
    square = (wide, wide)
    inputs = (x, e, metric)
    x_here, e_here, to_mate, to_outer, row = call(
        pack_kernel,
        [((c, n, lat), BF16)] * 2 + [halo] * 2 + [((1, lat), F32)],
        [((4, c, lat), BF16), ((lat,), F32), pltpu.SemaphoreType.DMA((3,))],
        *(pltpu.with_memory_space_constraint(a, pltpu.HBM) for a in inputs),
        specs=[pl.BlockSpec(memory_space=pltpu.HBM)] * len(inputs),
    )
    from_outer = exchange(to_outer, outers)
    from_mate = exchange(to_mate, mates)
    wide_columns = ((n,) + column, F32)
    pair = ((2, c, lat), F32)
    two = ((2, c, lat), BF16)
    two_wide = ((2,) + column, BF16)
    et, w1, w1a, w2a, g1, g2, d, s, fields, upstream, upstream_scaled, u, grad, y, z = call(
        interior_kernel,
        [turned_form]
        + [(square, BF16)] * 3
        + [(square, F32)] * 2
        + [turned_form] * 2
        + [((4,) + column, BF16)]
        + [two] * 2
        + [pair] * 4,
        [turned_form, ((n,) + column, BF16), turned_form]
        + [wide_columns] * 2
        + [((n,) + column, BF16)],
        x_here, e_here, kernel_first, kernel_second, row,
    )
    packed = (3 * wide // 2, 2 * c)
    common = (from_outer, from_mate, row, w1, w2a, g1, g2, fields, upstream, upstream_scaled)
    sent, *edge = call(
        edge_kernel, [(packed, BF16), two_wide, two, two, two, two_wide], [], *common, u, grad
    )
    near_fields, near_scaled, delta, delta_scaled, hidden = edge

    def keep(done, gate):
        return call(
            kept_kernel, [(packed, F32), two, two], [],
            *common, y, z, near_fields, near_scaled, delta, delta_scaled, gate(hidden),
        )

    def part(done, gate, start, count):
        return call(
            functools.partial(field_kernel, start=start),
            [((count, c, lat), BF16)],
            [((count + 2, c, lat), F32), ((count + 2, 2 * c, lat), F32)],
            et, d, s, delta, delta_scaled, done[0][1], done[0][2], gate(w1a),
        )

    def assemble(done, gate):
        return call(
            assemble_kernel, [((c, n, lat), BF16)], [], done[1][0], gate(done[2][0])
        )

    half = n // 2
    return sent, [
        keep,
        lambda done, gate: part(done, gate, 0, half),
        lambda done, gate: part(done, gate, half, n - half),
        assemble,
    ]


def sum_everywhere(sent, jobs, factor):
    dp, lon = lax.axis_size("dp"), lax.axis_size("lon")
    count = dp * lon
    swap = [(i, i ^ 1) for i in range(count)]
    jobs, done = list(jobs), []

    def beside(sent, pairs):
        got = exchange(sent, pairs)
        if jobs:
            result = jobs.pop(0)(done, lambda x: lax.optimization_barrier((sent, x))[1])
            got, first = lax.optimization_barrier((got, result[0]))
            done.append([first] + list(result[1:]))
        return got

    got = beside(sent, swap)
    total = done[0][0] + got.astype(F32)
    along_lon = [1 << k for k in range(1, lon.bit_length() - 1)]
    along_dp = [lon << k for k in range(dp.bit_length() - 1)]
    bits, other = along_lon + along_dp, along_dp + along_lon
    for even_bit, odd_bit in zip(bits, other):
        sent = total.astype(BF16)
        got = beside(
            sent, [(i, i ^ 1 ^ (odd_bit if i.bit_count() & 1 else even_bit)) for i in range(count)]
        )
        total = sent.astype(F32) + got.astype(F32)
    while jobs:
        done.append(jobs.pop(0)(done, lambda x: x))
    mine = (total * factor).astype(BF16)
    return mine, exchange(mine, swap), done


def per_device(fields, cotangent, kernel_first, kernel_second, metric):
    samples, c, n, lat = fields.shape
    counted = (
        float(samples * lax.axis_size("dp")) * float(n * lax.axis_size("lon")) * float(lat)
    )
    factor = jnp.float32(1.0 / counted**0.5)
    sent, jobs = one_sample(fields[0], cotangent[0], kernel_first, kernel_second, metric)
    mine, theirs, done = sum_everywhere(sent, jobs, factor)
    grad_first, grad_second = call(
        final_kernel, [((3, 3, c, c), BF16)] * 2, [], mine, theirs
    )
    return done[-1][0][None], grad_first, grad_second


def solution(mesh):
    placed = (P("dp", None, "lon", None), P("dp", None, "lon", None), P(), P(), P())
    return jax.shard_map(
        per_device,
        mesh=mesh,
        in_specs=placed,
        out_specs=(P("dp", None, "lon", None), P(), P()),
        check_vma=False,
    )
```

```python
import functools
import math

import jax
import jax.numpy as jnp
from jax import lax
from jax.experimental import pallas as pl
from jax.experimental.pallas import tpu as pltpu
from jax.sharding import PartitionSpec as P

gelu_coef = 0.7978845608
F32 = jnp.float32
BF16 = jnp.bfloat16
NT = (((1,), (1,)), ((), ()))


def gelu_pair(u):
    square = u * u
    inner = jnp.tanh(u * (gelu_coef + (gelu_coef * 0.044715) * square))
    a = 0.5 + 0.5 * inner
    value = u * a
    twice = 2.0 * gelu_coef + (6.0 * gelu_coef * 0.044715) * square
    return value, a + (value - value * a) * twice


def neighbours(v):
    lanes = 128
    tiles = [v[:, k : k + lanes] for k in range(0, v.shape[-1], lanes)]
    lane = lax.broadcasted_iota(jnp.int32, tiles[0].shape, 1)
    zero = jnp.zeros_like(tiles[0])
    up = [zero] + [pltpu.roll(t, 1, 1) for t in tiles]
    down = [pltpu.roll(t, lanes - 1, 1) for t in tiles] + [zero]
    below = [jnp.where(lane == 0, up[k], up[k + 1]) for k in range(len(tiles))]
    above = [jnp.where(lane == lanes - 1, down[k + 1], down[k]) for k in range(len(tiles))]
    return jnp.concatenate(below, axis=1), jnp.concatenate(above, axis=1)


def dot(a, b):
    return jnp.dot(a, b, preferred_element_type=F32)


def dot_nt(a, b):
    return lax.dot_general(a, b, NT, preferred_element_type=F32)


def three(v, adjoint):
    below, above = neighbours(v)
    return jnp.concatenate([above, v, below] if adjoint else [below, v, above], axis=0)


def prepare(k_ref, forward_ref, adjoint_ref):
    c = k_ref.shape[-1]
    for p in range(3):
        if forward_ref is not None:
            forward_ref[p * c : (p + 1) * c, :] = jnp.concatenate(
                [k_ref[p, q].astype(F32) for q in range(3)], axis=1
            ).astype(BF16)
        adjoint_ref[p * c : (p + 1) * c, :] = jnp.concatenate(
            [k_ref[p, q].astype(F32).T for q in range(3)], axis=1
        ).astype(BF16)


def products(i, w1, w2a, x3, e3, s3, y, z):
    c = w1.shape[0] // 3
    y[i] = dot(w1[...], x3)
    z[i, c : 2 * c, :] = dot(w2a[c : 2 * c, :], e3)
    sides = dot(jnp.concatenate([w2a[0:c, :], w2a[2 * c :, :]], axis=0), s3)
    z[i, 0:c, :] = sides[0:c]
    z[i, 2 * c :, :] = sides[c:]


def middle(u, grad, metric):
    hidden, slope = gelu_pair(u)
    delta = (grad * slope).astype(BF16)
    return hidden.astype(BF16), delta, (metric * delta.astype(F32)).astype(BF16)


def edges_term(
    t, fields, upstream, upstream_scaled, near_fields, near_scaled, delta, delta_scaled, hidden
):
    first = t == 0
    rows = []
    for p in range(3):
        left, right = [], []
        for side, (own, inner) in enumerate(((0, 1), (3, 2))):
            if p == 1:
                one, two, three_fields = delta[side], upstream[side], fields[own]
            else:
                one = delta_scaled[side]
                if (p == 0) == (side == 0):
                    two, three_fields = upstream_scaled[side], near_fields[side]
                else:
                    two, three_fields = near_scaled[side], fields[inner]
            left.append(jnp.where(first, one, two))
            right.append(jnp.where(first, three_fields, hidden[side]))
        rows.append(dot_nt(jnp.concatenate(left, axis=1), jnp.concatenate(right, axis=1)))
    return jnp.concatenate(rows, axis=0)


def put_packed(ref, total):
    half = total.shape[0] // 2
    wide = total.shape[1] // 3 * 2
    tail = total[:, wide:]
    ref[0 : 2 * half, :] = total[:, 0:wide].astype(ref.dtype)
    ref[2 * half :, :] = jnp.concatenate([tail[0:half], tail[half:]], axis=1).astype(ref.dtype)


def turning(n, back=False, odd=None):
    shape = (16 * n if odd is None else 64, 16 * n)
    row = lax.broadcasted_iota(jnp.int32, shape, 1 if back else 0)
    source = lax.broadcasted_iota(jnp.int32, shape, 0 if back else 1)
    place = lax.shift_right_logical(row, jnp.full_like(row, 4))
    if odd is not None:
        mate = jnp.where(odd, 0, n - 2)
        place = jnp.where(place < 2, place + mate, place - 2 + (n - 2 - mate))
    return jnp.where(source == (row & 15) * n + place, 1.0, 0.0).astype(BF16)


def turn_columns(turn, source, target):
    c, n, lat = source.shape
    for b in range(0, c, 16):
        turned = dot(turn, source[b : b + 16].reshape(16 * n, lat)).astype(BF16)
        for i in range(turn.shape[0] // 16):
            target(i)[b : b + 16, :] = turned[16 * i : 16 * (i + 1)]


def pack_kernel(
    x_hbm, e_hbm, m_hbm, x_ref, e_ref, mate_ref, outer_ref, row_ref, ms, sems
):
    n, lat = x_hbm.shape[1:]
    copies = [
        pltpu.make_async_copy(src, dst, sems.at[a])
        for a, (src, dst) in enumerate(((x_hbm, x_ref), (e_hbm, e_ref), (m_hbm, ms)))
    ]
    for copy in copies:
        copy.start()
    turn = turning(n, odd=lax.axis_index("lon") % 2 == 1)
    for a, source in enumerate((x_ref, e_ref)):
        copies[a].wait()
        turn_columns(
            turn, source, lambda i, a=a: mate_ref.at[a, i] if i < 2 else outer_ref.at[a, i - 2]
        )
    copies[2].wait()
    row_ref[...] = ms[...].reshape(1, lat)


def interior_kernel(
    x_ref, e_ref, k1_ref, k2_ref, m_ref,
    e, w1_ref, w1a_ref, w2a_ref, g1_ref, g2_ref, d_ref, s_ref, fields, upstream, upstream_scaled, u_ref, grad_ref, y_ref, z_ref,
    x, x3, es, y, z, h3,
):
    n, c, lat = d_ref.shape
    low, mid, high = slice(0, c), slice(c, 2 * c), slice(2 * c, 3 * c)
    metric = m_ref[...]
    turn = turning(n)
    turn_columns(turn, x_ref, lambda i: x.at[i])
    turn_columns(turn, e_ref, lambda i: e.at[i])
    prepare(k1_ref, w1_ref, w1a_ref)
    prepare(k2_ref, None, w2a_ref)
    blank = jnp.zeros((c, lat), BF16)
    for i in (0, n - 1):
        d_ref[i] = blank
        s_ref[i] = blank
    g1_ref[...] = jnp.zeros_like(g1_ref)
    g2_ref[...] = jnp.zeros_like(g2_ref)

    def terms(plain, scaled, value, columns):
        left = [jnp.concatenate([scaled[j + 1], plain[j], scaled[j - 1]], axis=0) for j in columns]
        return dot_nt(
            jnp.concatenate(left, axis=1), jnp.concatenate([value[j] for j in columns], axis=1)
        )

    inner = list(range(1, n - 1))
    groups = [inner[k : k + 7] for k in range(0, n - 2, 7)]
    second_todo, first_todo = list(groups), list(groups)
    for i in range(n + 1):
        if i < n:
            x3[i] = three(x[i], False)
            es[i] = (metric * e[i].astype(F32)).astype(BF16)
            products(i, w1_ref, w2a_ref, x3[i], three(e[i], True), three(es[i], True), y, z)
        k = i - 1
        if 0 < k < n - 1:
            u = y[k, mid, :] + metric * (y[k - 1, low, :] + y[k + 1, high, :])
            grad = z[k, mid, :] + (z[k + 1, low, :] + z[k - 1, high, :])
            hidden, delta, scaled = middle(u, grad, metric)
            h3[k] = three(hidden, False)
            d_ref[k] = delta
            s_ref[k] = scaled
        if i == 3:
            g1_ref[0:c, :] += dot_nt(s_ref[1], x3[0])
        ready = i - 2 if i < n else n - 2
        if second_todo and second_todo[0][-1] <= ready:
            g2_ref[...] += terms(e, es, h3, second_todo.pop(0))
        if first_todo and first_todo[0][-1] <= (ready - 1 if i < n else ready):
            g1_ref[...] += terms(d_ref, s_ref, x3, first_todo.pop(0))
    g1_ref[2 * c :, :] += dot_nt(s_ref[n - 2], x3[n - 1])
    for side, own, next_in, one, two in ((0, 0, 1, low, high), (1, n - 1, n - 2, high, low)):
        u_ref[side] = y[own, mid, :] + metric * y[next_in, two, :]
        grad_ref[side] = z[own, mid, :] + z[next_in, one, :]
        y_ref[side] = y[own, two, :]
        z_ref[side] = z[own, one, :]
        upstream[side] = e[own]
        upstream_scaled[side] = es[next_in]
    for k, i in enumerate((0, 1, n - 2, n - 1)):
        fields[k] = x3[i]


def parity():
    place = lax.axis_index("dp") * lax.axis_size("lon") + lax.axis_index("lon")
    total, left = 0, lax.axis_size("dp") * lax.axis_size("lon") - 1
    while left:
        total, place, left = total + place % 2, place // 2, left // 2
    return total % 2


def beyond(odd, from_mate, from_outer, side, array, distance):
    k = distance - 1 if side else 2 - distance
    low_is_mate = jnp.where(odd, from_mate[array, k], from_outer[array, k])
    high_is_mate = jnp.where(odd, from_outer[array, k], from_mate[array, k])
    return high_is_mate if side else low_is_mate


def edge_kernel(
    from_outer, from_mate, m_ref, w1, w2a, g1, g2, fields, upstream, upstream_scaled, u_ref, grad_ref,
    sent_ref, near_fields, near_scaled, delta, delta_scaled, hidden,
):
    metric = m_ref[...]
    c = from_mate.shape[2]
    low, high = slice(0, c), slice(2 * c, 3 * c)
    odd = lax.axis_index("lon") % 2 == 1
    t = 1 - parity()
    for side, one, two in ((0, low, high), (1, high, low)):
        x, e = (beyond(odd, from_mate, from_outer, side, a, 1) for a in range(2))
        near_fields[side] = three(x, False)
        near_scaled[side] = (metric * e.astype(F32)).astype(BF16)
        u = u_ref[side] + metric * dot(w1[one, :], near_fields[side])
        grad = grad_ref[side] + dot(w2a[two, :], three(near_scaled[side], True))
        h, delta[side], delta_scaled[side] = middle(u, grad, metric)
        hidden[side] = three(h, False)
    total = edges_term(
        t, fields, upstream, upstream_scaled, near_fields, near_scaled, delta, delta_scaled, hidden
    )
    put_packed(sent_ref, total + jnp.where(t == 0, g1[...], g2[...]))


def kept_kernel(
    from_outer, from_mate, m_ref, w1, w2a, g1, g2, fields, upstream, upstream_scaled, y_ref, z_ref,
    near_fields, near_scaled, delta, delta_scaled, hidden,
    kept_ref, near_delta, near_delta_scaled,
):
    metric = m_ref[...]
    c = from_mate.shape[2]
    low, mid, high = slice(0, c), slice(c, 2 * c), slice(2 * c, 3 * c)
    odd = lax.axis_index("lon") % 2 == 1
    t = parity()
    total = edges_term(
        t, fields, upstream, upstream_scaled, near_fields, near_scaled, delta, delta_scaled, hidden
    )
    put_packed(kept_ref, total + jnp.where(t == 0, g1[...], g2[...]))
    for side, one, two in ((0, low, high), (1, high, low)):
        x, e = (beyond(odd, from_mate, from_outer, side, a, 2) for a in range(2))
        near_e = beyond(odd, from_mate, from_outer, side, 1, 1)
        scaled = (metric * e.astype(F32)).astype(BF16)
        u = dot(w1[mid, :], near_fields[side]) + metric * (
            dot(w1[one, :], three(x, False)) + y_ref[side]
        )
        grad = dot(w2a[mid, :], three(near_e, True)) + (
            dot(w2a[two, :], three(scaled, True)) + z_ref[side]
        )
        _, near_delta[side], near_delta_scaled[side] = middle(u, grad, metric)


def field_kernel(
    e_ref, d_in, s_in, delta, delta_scaled, near_delta, near_delta_scaled, w1a_ref, out_ref, zm, zs, *, start
):
    c, n = d_in.shape[1], d_in.shape[0]
    count = out_ref.shape[0]
    sides = jnp.concatenate([w1a_ref[0:c, :], w1a_ref[2 * c :, :]], axis=0)
    edges = {
        -1: (near_delta, near_delta_scaled, 0),
        0: (delta, delta_scaled, 0),
        n - 1: (delta, delta_scaled, 1),
        n: (near_delta, near_delta_scaled, 1),
    }
    for place in range(count + 2):
        i = start + place - 1
        plain, scaled, k = edges.get(i, (d_in, s_in, i))
        if 0 < place < count + 1:
            zm[place] = dot(w1a_ref[c : 2 * c, :], three(plain[k], True))
        zs[place] = dot(sides, three(scaled[k], True))
        if place >= 2:
            grad = zm[place - 1] + (zs[place, 0:c, :] + zs[place - 2, c:, :])
            out_ref[place - 2] = (e_ref[i - 1].astype(F32) + grad).astype(BF16)


def assemble_kernel(*refs):
    parts, out_ref = refs[:-1], refs[-1]
    c, n, lat = out_ref.shape
    turn = turning(n, back=True)
    for b in range(0, c, 16):
        rows = [part[k, b : b + 16, :] for part in parts for k in range(part.shape[0])]
        turned = dot(turn, jnp.concatenate(rows, axis=0))
        out_ref[b : b + 16] = turned.astype(BF16).reshape(16, n, lat)


def final_kernel(mine_ref, theirs_ref, out1_ref, out2_ref):
    c = out1_ref.shape[-1]
    odd = parity() == 1
    mine, theirs = mine_ref[...], theirs_ref[...]
    for out, packed in (
        (out1_ref, jnp.where(odd, theirs, mine)),
        (out2_ref, jnp.where(odd, mine, theirs)),
    ):
        tail = packed[3 * c :]
        tail = jnp.concatenate([tail[:, 0:c], tail[:, c:]], axis=0)
        for p in range(3):
            rows = slice(p * c, (p + 1) * c)
            out[p, 0] = packed[rows, 0:c]
            out[p, 1] = packed[rows, c:]
            out[p, 2] = tail[rows]


def vmem(count):
    return [pl.BlockSpec(memory_space=pltpu.VMEM)] * count


def size_of(shapes):
    return sum(math.prod(s) * jnp.dtype(d).itemsize for s, d in shapes)


def call(kernel, outs, scratch, *args, specs=None):
    mib = 2**20
    buffers = [s for s in scratch if isinstance(s, tuple)]
    limit = size_of(buffers) + size_of(outs) + size_of([(a.shape, a.dtype) for a in args])
    return pl.pallas_call(
        kernel,
        out_shape=[jax.ShapeDtypeStruct(s, d) for s, d in outs],
        in_specs=specs or vmem(len(args)),
        out_specs=vmem(len(outs)),
        scratch_shapes=[pltpu.VMEM(*s) if isinstance(s, tuple) else s for s in scratch],
        compiler_params=pltpu.CompilerParams(vmem_limit_bytes=(limit // mib + 6) * mib),
    )(*args)


def exchange(value, pairs):
    return lax.ppermute(value, ("dp", "lon"), pairs)


def one_sample(x, e, kernel_first, kernel_second, metric):
    c, n, lat = x.shape
    wide = 3 * c
    count = lax.axis_size("dp") * lax.axis_size("lon")
    lon = lax.axis_size("lon")
    mates = [(i, i ^ 1) for i in range(count)]
    outers = [
        (i, i // lon * lon + (i % lon + (1 if i % lon % 2 else -1)) % lon) for i in range(count)
    ]
    turned_form = ((n, c, lat), BF16)
    column = (wide, lat)
    halo = ((2, 2, c, lat), BF16)
    square = (wide, wide)
    inputs = (x, e, metric)
    x_here, e_here, to_mate, to_outer, row = call(
        pack_kernel,
        [((c, n, lat), BF16)] * 2 + [halo] * 2 + [((1, lat), F32)],
        [((lat,), F32), pltpu.SemaphoreType.DMA((3,))],
        *(pltpu.with_memory_space_constraint(a, pltpu.HBM) for a in inputs),
        specs=[pl.BlockSpec(memory_space=pltpu.HBM)] * len(inputs),
    )
    from_outer = exchange(to_outer, outers)
    from_mate = exchange(to_mate, mates)
    wide_columns = ((n,) + column, F32)
    pair = ((2, c, lat), F32)
    two = ((2, c, lat), BF16)
    two_wide = ((2,) + column, BF16)
    et, w1, w1a, w2a, g1, g2, d, s, fields, upstream, upstream_scaled, u, grad, y, z = call(
        interior_kernel,
        [turned_form]
        + [(square, BF16)] * 3
        + [(square, F32)] * 2
        + [turned_form] * 2
        + [((4,) + column, BF16)]
        + [two] * 2
        + [pair] * 4,
        [turned_form, ((n,) + column, BF16), turned_form]
        + [wide_columns] * 2
        + [((n,) + column, BF16)],
        x_here, e_here, kernel_first, kernel_second, row,
    )
    packed = (3 * wide // 2, 2 * c)
    common = (from_outer, from_mate, row, w1, w2a, g1, g2, fields, upstream, upstream_scaled)
    sent, *edge = call(
        edge_kernel, [(packed, BF16), two_wide, two, two, two, two_wide], [], *common, u, grad
    )
    near_fields, near_scaled, delta, delta_scaled, hidden = edge

    def keep(done, gate):
        return call(
            kept_kernel, [(packed, F32), two, two], [],
            *common, y, z, near_fields, near_scaled, delta, delta_scaled, gate(hidden),
        )

    def part(done, gate, start, count):
        return call(
            functools.partial(field_kernel, start=start),
            [((count, c, lat), BF16)],
            [((count + 2, c, lat), F32), ((count + 2, 2 * c, lat), F32)],
            et, d, s, delta, delta_scaled, done[0][1], done[0][2], gate(w1a),
        )

    def assemble(done, gate):
        return call(
            assemble_kernel, [((c, n, lat), BF16)], [], done[1][0], gate(done[2][0])
        )

    half = n // 2
    return sent, [
        keep,
        lambda done, gate: part(done, gate, 0, half),
        lambda done, gate: part(done, gate, half, n - half),
        assemble,
    ]


def sum_everywhere(sent, jobs, factor):
    dp, lon = lax.axis_size("dp"), lax.axis_size("lon")
    count = dp * lon
    swap = [(i, i ^ 1) for i in range(count)]
    jobs, done = list(jobs), []

    def beside(sent, pairs):
        got = exchange(sent, pairs)
        if jobs:
            result = jobs.pop(0)(done, lambda x: lax.optimization_barrier((sent, x))[1])
            got, first = lax.optimization_barrier((got, result[0]))
            done.append([first] + list(result[1:]))
        return got

    got = beside(sent, swap)
    total = done[0][0] + got.astype(F32)
    along_lon = [1 << k for k in range(1, lon.bit_length() - 1)]
    along_dp = [lon << k for k in range(dp.bit_length() - 1)]
    bits, other = along_lon + along_dp, along_dp + along_lon
    for even_bit, odd_bit in zip(bits, other):
        sent = total.astype(BF16)
        got = beside(
            sent, [(i, i ^ 1 ^ (odd_bit if i.bit_count() & 1 else even_bit)) for i in range(count)]
        )
        total = sent.astype(F32) + got.astype(F32)
    while jobs:
        done.append(jobs.pop(0)(done, lambda x: x))
    mine = (total * factor).astype(BF16)
    return mine, exchange(mine, swap), done


def per_device(fields, cotangent, kernel_first, kernel_second, metric):
    samples, c, n, lat = fields.shape
    counted = (
        float(samples * lax.axis_size("dp")) * float(n * lax.axis_size("lon")) * float(lat)
    )
    factor = jnp.float32(1.0 / counted**0.5)
    sent, jobs = one_sample(fields[0], cotangent[0], kernel_first, kernel_second, metric)
    mine, theirs, done = sum_everywhere(sent, jobs, factor)
    grad_first, grad_second = call(
        final_kernel, [((3, 3, c, c), BF16)] * 2, [], mine, theirs
    )
    return done[-1][0][None], grad_first, grad_second


def solution(mesh):
    placed = (P("dp", None, "lon", None), P("dp", None, "lon", None), P(), P(), P())
    return jax.shard_map(
        per_device,
        mesh=mesh,
        in_specs=placed,
        out_specs=(P("dp", None, "lon", None), P(), P()),
        check_vma=False,
    )
```

```python
import functools
import math

import jax
import jax.numpy as jnp
from jax import lax
from jax.experimental import pallas as pl
from jax.experimental.pallas import tpu as pltpu
from jax.sharding import PartitionSpec as P

gelu_coef = 0.7978845608
F32 = jnp.float32
BF16 = jnp.bfloat16
NT = (((1,), (1,)), ((), ()))


def gelu_pair(u):
    square = u * u
    inner = jnp.tanh(u * (gelu_coef + (gelu_coef * 0.044715) * square))
    a = 0.5 + 0.5 * inner
    value = u * a
    twice = 2.0 * gelu_coef + (6.0 * gelu_coef * 0.044715) * square
    return value, a + (value - value * a) * twice


def neighbours(v):
    lanes = 128
    tiles = [v[:, k : k + lanes] for k in range(0, v.shape[-1], lanes)]
    lane = lax.broadcasted_iota(jnp.int32, tiles[0].shape, 1)
    zero = jnp.zeros_like(tiles[0])
    up = [zero] + [pltpu.roll(t, 1, 1) for t in tiles]
    down = [pltpu.roll(t, lanes - 1, 1) for t in tiles] + [zero]
    below = [jnp.where(lane == 0, up[k], up[k + 1]) for k in range(len(tiles))]
    above = [jnp.where(lane == lanes - 1, down[k + 1], down[k]) for k in range(len(tiles))]
    return jnp.concatenate(below, axis=1), jnp.concatenate(above, axis=1)


def dot(a, b):
    return jnp.dot(a, b, preferred_element_type=F32)


def dot_nt(a, b):
    return lax.dot_general(a, b, NT, preferred_element_type=F32)


def three(v, adjoint):
    below, above = neighbours(v)
    return jnp.concatenate([above, v, below] if adjoint else [below, v, above], axis=0)


def prepare(k_ref, forward_ref=None, adjoint_ref=None):
    c = k_ref.shape[-1]
    for p in range(3):
        if forward_ref is not None:
            forward_ref[p * c : (p + 1) * c, :] = jnp.concatenate(
                [k_ref[p, q].astype(F32) for q in range(3)], axis=1
            ).astype(BF16)
        if adjoint_ref is not None:
            adjoint_ref[p * c : (p + 1) * c, :] = jnp.concatenate(
                [k_ref[p, q].astype(F32).T for q in range(3)], axis=1
            ).astype(BF16)


def products(i, w1, w2a, x3, e3, s3, y, z):
    c = w1.shape[0] // 3
    y[i] = dot(w1[...], x3)
    z[i, c : 2 * c, :] = dot(w2a[c : 2 * c, :], e3)
    sides = dot(jnp.concatenate([w2a[0:c, :], w2a[2 * c :, :]], axis=0), s3)
    z[i, 0:c, :] = sides[0:c]
    z[i, 2 * c :, :] = sides[c:]


def middle(u, grad, metric):
    hidden, slope = gelu_pair(u)
    delta = (grad * slope).astype(BF16)
    return hidden.astype(BF16), delta, (metric * delta.astype(F32)).astype(BF16)


def edges_term(
    t, fields, upstream, upstream_scaled, near_fields, near_scaled, delta, delta_scaled, hidden
):
    first = t == 0
    rows = []
    for p in range(3):
        left, right = [], []
        for side, (own, inner) in enumerate(((0, 1), (3, 2))):
            if p == 1:
                one, two, three_fields = delta[side], upstream[side], fields[own]
            else:
                one = delta_scaled[side]
                if (p == 0) == (side == 0):
                    two, three_fields = upstream_scaled[side], near_fields[side]
                else:
                    two, three_fields = near_scaled[side], fields[inner]
            left.append(jnp.where(first, one, two))
            right.append(jnp.where(first, three_fields, hidden[side]))
        rows.append(dot_nt(jnp.concatenate(left, axis=1), jnp.concatenate(right, axis=1)))
    return jnp.concatenate(rows, axis=0)


def put_packed(ref, total):
    half = total.shape[0] // 2
    wide = total.shape[1] // 3 * 2
    tail = total[:, wide:]
    ref[0 : 2 * half, :] = total[:, 0:wide].astype(ref.dtype)
    ref[2 * half :, :] = jnp.concatenate([tail[0:half], tail[half:]], axis=1).astype(ref.dtype)


def turning(n, back=False, edges=False):
    shape = (64 if edges else 16 * n, 16 * n)
    row = lax.broadcasted_iota(jnp.int32, shape, 1 if back else 0)
    source = lax.broadcasted_iota(jnp.int32, shape, 0 if back else 1)
    place = lax.shift_right_logical(row, jnp.full_like(row, 4))
    if edges:
        place = jnp.where(place < 2, place, place + n - 4)
    return jnp.where(source == (row & 15) * n + place, 1.0, 0.0).astype(BF16)


def turn_columns(turn, source, target):
    c, n, lat = source.shape
    for b in range(0, c, 16):
        turned = dot(turn, source[b : b + 16].reshape(16 * n, lat)).astype(BF16)
        for i in range(turn.shape[0] // 16):
            target[i, b : b + 16, :] = turned[16 * i : 16 * (i + 1)]


def pack_kernel(
    x_hbm, e_hbm, m_hbm, x_ref, e_ref, mate_ref, outer_ref, row_ref, edges, ms, sems
):
    n, lat = x_hbm.shape[1:]
    copies = [
        pltpu.make_async_copy(src, dst, sems.at[a])
        for a, (src, dst) in enumerate(((x_hbm, x_ref), (e_hbm, e_ref), (m_hbm, ms)))
    ]
    for copy in copies:
        copy.start()
    turn = turning(n, edges=True)
    odd = lax.axis_index("lon") % 2 == 1
    for a, source in enumerate((x_ref, e_ref)):
        copies[a].wait()
        turn_columns(turn, source, edges)
        for k in range(2):
            mate_ref[a, k] = jnp.where(odd, edges[k], edges[2 + k])
            outer_ref[a, k] = jnp.where(odd, edges[2 + k], edges[k])
    copies[2].wait()
    row_ref[...] = ms[...].reshape(1, lat)


def interior_kernel(
    x_ref, e_ref, k1_ref, k2_ref, m_ref,
    e, w1_ref, w2a_ref, g1_ref, g2_ref, d_ref, s_ref, fields, upstream, upstream_scaled, u_ref, grad_ref, y_ref, z_ref,
    x, x3, es, y, z, h3,
):
    n, c, lat = d_ref.shape
    low, mid, high = slice(0, c), slice(c, 2 * c), slice(2 * c, 3 * c)
    metric = m_ref[...]
    turn = turning(n)
    turn_columns(turn, x_ref, x)
    turn_columns(turn, e_ref, e)
    prepare(k1_ref, forward_ref=w1_ref)
    prepare(k2_ref, adjoint_ref=w2a_ref)
    blank = jnp.zeros((c, lat), BF16)
    for i in (0, n - 1):
        d_ref[i] = blank
        s_ref[i] = blank
    g1_ref[...] = jnp.zeros_like(g1_ref)
    g2_ref[...] = jnp.zeros_like(g2_ref)

    def terms(plain, scaled, value, columns):
        left = [jnp.concatenate([scaled[j + 1], plain[j], scaled[j - 1]], axis=0) for j in columns]
        return dot_nt(
            jnp.concatenate(left, axis=1), jnp.concatenate([value[j] for j in columns], axis=1)
        )

    inner = list(range(1, n - 1))
    groups = [inner[k : k + 7] for k in range(0, n - 2, 7)]
    second_todo, first_todo = list(groups), list(groups)
    for i in range(n + 1):
        if i < n:
            x3[i] = three(x[i], False)
            es[i] = (metric * e[i].astype(F32)).astype(BF16)
            products(i, w1_ref, w2a_ref, x3[i], three(e[i], True), three(es[i], True), y, z)
        k = i - 1
        if 0 < k < n - 1:
            u = y[k, mid, :] + metric * (y[k - 1, low, :] + y[k + 1, high, :])
            grad = z[k, mid, :] + (z[k + 1, low, :] + z[k - 1, high, :])
            hidden, delta, scaled = middle(u, grad, metric)
            h3[k] = three(hidden, False)
            d_ref[k] = delta
            s_ref[k] = scaled
        if i == 3:
            g1_ref[0:c, :] += dot_nt(s_ref[1], x3[0])
        ready = i - 2 if i < n else n - 2
        if second_todo and second_todo[0][-1] <= ready:
            g2_ref[...] += terms(e, es, h3, second_todo.pop(0))
        if first_todo and first_todo[0][-1] <= (ready - 1 if i < n else ready):
            g1_ref[...] += terms(d_ref, s_ref, x3, first_todo.pop(0))
    g1_ref[2 * c :, :] += dot_nt(s_ref[n - 2], x3[n - 1])
    for side, own, next_in, one, two in ((0, 0, 1, low, high), (1, n - 1, n - 2, high, low)):
        u_ref[side] = y[own, mid, :] + metric * y[next_in, two, :]
        grad_ref[side] = z[own, mid, :] + z[next_in, one, :]
        y_ref[side] = y[own, two, :]
        z_ref[side] = z[own, one, :]
        upstream[side] = e[own]
        upstream_scaled[side] = es[next_in]
    for k, i in enumerate((0, 1, n - 2, n - 1)):
        fields[k] = x3[i]


def parity():
    place = lax.axis_index("dp") * lax.axis_size("lon") + lax.axis_index("lon")
    total, left = 0, lax.axis_size("dp") * lax.axis_size("lon") - 1
    while left:
        total, place, left = total + place % 2, place // 2, left // 2
    return total % 2


def beyond(odd, from_mate, from_outer, side, array, distance):
    k = distance - 1 if side else 2 - distance
    low_is_mate = jnp.where(odd, from_mate[array, k], from_outer[array, k])
    high_is_mate = jnp.where(odd, from_outer[array, k], from_mate[array, k])
    return high_is_mate if side else low_is_mate


def edge_kernel(
    from_outer, from_mate, m_ref, w1, w2a, g1, g2, fields, upstream, upstream_scaled, u_ref, grad_ref,
    sent_ref, near_fields, near_scaled, delta, delta_scaled, hidden,
):
    metric = m_ref[...]
    c = from_mate.shape[2]
    low, high = slice(0, c), slice(2 * c, 3 * c)
    odd = lax.axis_index("lon") % 2 == 1
    t = 1 - parity()
    for side, one, two in ((0, low, high), (1, high, low)):
        x, e = (beyond(odd, from_mate, from_outer, side, a, 1) for a in range(2))
        near_fields[side] = three(x, False)
        near_scaled[side] = (metric * e.astype(F32)).astype(BF16)
        u = u_ref[side] + metric * dot(w1[one, :], near_fields[side])
        grad = grad_ref[side] + dot(w2a[two, :], three(near_scaled[side], True))
        h, delta[side], delta_scaled[side] = middle(u, grad, metric)
        hidden[side] = three(h, False)
    total = edges_term(
        t, fields, upstream, upstream_scaled, near_fields, near_scaled, delta, delta_scaled, hidden
    )
    put_packed(sent_ref, total + jnp.where(t == 0, g1[...], g2[...]))


def kept_kernel(
    from_outer, from_mate, m_ref, w1, w2a, g1, g2, fields, upstream, upstream_scaled, y_ref, z_ref,
    near_fields, near_scaled, delta, delta_scaled, hidden, k1_ref,
    kept_ref, near_delta, near_delta_scaled, w1a_ref,
):
    metric = m_ref[...]
    c = from_mate.shape[2]
    low, mid, high = slice(0, c), slice(c, 2 * c), slice(2 * c, 3 * c)
    odd = lax.axis_index("lon") % 2 == 1
    t = parity()
    total = edges_term(
        t, fields, upstream, upstream_scaled, near_fields, near_scaled, delta, delta_scaled, hidden
    )
    put_packed(kept_ref, total + jnp.where(t == 0, g1[...], g2[...]))
    prepare(k1_ref, adjoint_ref=w1a_ref)
    for side, one, two in ((0, low, high), (1, high, low)):
        x, e = (beyond(odd, from_mate, from_outer, side, a, 2) for a in range(2))
        near_e = beyond(odd, from_mate, from_outer, side, 1, 1)
        scaled = (metric * e.astype(F32)).astype(BF16)
        u = dot(w1[mid, :], near_fields[side]) + metric * (
            dot(w1[one, :], three(x, False)) + y_ref[side]
        )
        grad = dot(w2a[mid, :], three(near_e, True)) + (
            dot(w2a[two, :], three(scaled, True)) + z_ref[side]
        )
        _, near_delta[side], near_delta_scaled[side] = middle(u, grad, metric)


def field_kernel(
    e_ref, d_in, s_in, delta, delta_scaled, near_delta, near_delta_scaled, w1a_ref, out_ref, zm, zs, *, start
):
    c, n = d_in.shape[1], d_in.shape[0]
    count = out_ref.shape[0]
    sides = jnp.concatenate([w1a_ref[0:c, :], w1a_ref[2 * c :, :]], axis=0)
    edges = {
        -1: (near_delta, near_delta_scaled, 0),
        0: (delta, delta_scaled, 0),
        n - 1: (delta, delta_scaled, 1),
        n: (near_delta, near_delta_scaled, 1),
    }
    for place in range(count + 2):
        i = start + place - 1
        plain, scaled, k = edges.get(i, (d_in, s_in, i))
        if 0 < place < count + 1:
            zm[place] = dot(w1a_ref[c : 2 * c, :], three(plain[k], True))
        zs[place] = dot(sides, three(scaled[k], True))
        if place >= 2:
            grad = zm[place - 1] + (zs[place, 0:c, :] + zs[place - 2, c:, :])
            out_ref[place - 2] = (e_ref[i - 1].astype(F32) + grad).astype(BF16)


def assemble_kernel(*refs):
    parts, out_ref = refs[:-1], refs[-1]
    c, n, lat = out_ref.shape
    turn = turning(n, back=True)
    for b in range(0, c, 16):
        rows = [part[k, b : b + 16, :] for part in parts for k in range(part.shape[0])]
        turned = dot(turn, jnp.concatenate(rows, axis=0))
        out_ref[b : b + 16] = turned.astype(BF16).reshape(16, n, lat)


def final_kernel(mine_ref, theirs_ref, out1_ref, out2_ref):
    c = out1_ref.shape[-1]
    odd = parity() == 1
    mine, theirs = mine_ref[...], theirs_ref[...]
    for out, packed in (
        (out1_ref, jnp.where(odd, theirs, mine)),
        (out2_ref, jnp.where(odd, mine, theirs)),
    ):
        tail = packed[3 * c :]
        tail = jnp.concatenate([tail[:, 0:c], tail[:, c:]], axis=0)
        for p in range(3):
            rows = slice(p * c, (p + 1) * c)
            out[p, 0] = packed[rows, 0:c]
            out[p, 1] = packed[rows, c:]
            out[p, 2] = tail[rows]


def vmem(count):
    return [pl.BlockSpec(memory_space=pltpu.VMEM)] * count


def size_of(shapes):
    return sum(math.prod(s) * jnp.dtype(d).itemsize for s, d in shapes)


def call(kernel, outs, scratch, *args, specs=None):
    mib = 2**20
    buffers = [s for s in scratch if isinstance(s, tuple)]
    limit = size_of(buffers) + size_of(outs) + size_of([(a.shape, a.dtype) for a in args])
    return pl.pallas_call(
        kernel,
        out_shape=[jax.ShapeDtypeStruct(s, d) for s, d in outs],
        in_specs=specs or vmem(len(args)),
        out_specs=vmem(len(outs)),
        scratch_shapes=[pltpu.VMEM(*s) if isinstance(s, tuple) else s for s in scratch],
        compiler_params=pltpu.CompilerParams(vmem_limit_bytes=(limit // mib + 6) * mib),
    )(*args)


def exchange(value, pairs):
    return lax.ppermute(value, ("dp", "lon"), pairs)


def one_sample(x, e, kernel_first, kernel_second, metric):
    c, n, lat = x.shape
    wide = 3 * c
    count = lax.axis_size("dp") * lax.axis_size("lon")
    lon = lax.axis_size("lon")
    mates = [(i, i ^ 1) for i in range(count)]
    outers = [
        (i, i // lon * lon + (i % lon + (1 if i % lon % 2 else -1)) % lon) for i in range(count)
    ]
    turned_form = ((n, c, lat), BF16)
    column = (wide, lat)
    halo = ((2, 2, c, lat), BF16)
    square = (wide, wide)
    inputs = (x, e, metric)
    x_here, e_here, to_mate, to_outer, row = call(
        pack_kernel,
        [((c, n, lat), BF16)] * 2 + [halo] * 2 + [((1, lat), F32)],
        [((4, c, lat), BF16), ((lat,), F32), pltpu.SemaphoreType.DMA((3,))],
        *(pltpu.with_memory_space_constraint(a, pltpu.HBM) for a in inputs),
        specs=[pl.BlockSpec(memory_space=pltpu.HBM)] * len(inputs),
    )
    from_outer = exchange(to_outer, outers)
    from_mate = exchange(to_mate, mates)
    wide_columns = ((n,) + column, F32)
    pair = ((2, c, lat), F32)
    two = ((2, c, lat), BF16)
    two_wide = ((2,) + column, BF16)
    et, w1, w2a, g1, g2, d, s, fields, upstream, upstream_scaled, u, grad, y, z = call(
        interior_kernel,
        [turned_form]
        + [(square, BF16)] * 2
        + [(square, F32)] * 2
        + [turned_form] * 2
        + [((4,) + column, BF16)]
        + [two] * 2
        + [pair] * 4,
        [turned_form, ((n,) + column, BF16), turned_form]
        + [wide_columns] * 2
        + [((n,) + column, BF16)],
        x_here, e_here, kernel_first, kernel_second, row,
    )
    packed = (3 * wide // 2, 2 * c)
    common = (from_outer, from_mate, row, w1, w2a, g1, g2, fields, upstream, upstream_scaled)
    sent, *edge = call(
        edge_kernel, [(packed, BF16), two_wide, two, two, two, two_wide], [], *common, u, grad
    )
    near_fields, near_scaled, delta, delta_scaled, hidden = edge

    def keep(done, gate):
        return call(
            kept_kernel, [(packed, F32), two, two, (square, BF16)], [],
            *common, y, z, near_fields, near_scaled, delta, delta_scaled, gate(hidden), kernel_first,
        )

    def part(done, gate, start, count):
        return call(
            functools.partial(field_kernel, start=start),
            [((count, c, lat), BF16)],
            [((count + 2, c, lat), F32), ((count + 2, 2 * c, lat), F32)],
            et, d, s, delta, delta_scaled, done[0][1], done[0][2], gate(done[0][3]),
        )

    def assemble(done, gate):
        return call(
            assemble_kernel, [((c, n, lat), BF16)], [], done[1][0], gate(done[2][0])
        )

    half = n // 2
    return sent, [
        keep,
        lambda done, gate: part(done, gate, 0, half),
        lambda done, gate: part(done, gate, half, n - half),
        assemble,
    ]


def sum_everywhere(sent, jobs, factor):
    dp, lon = lax.axis_size("dp"), lax.axis_size("lon")
    count = dp * lon
    swap = [(i, i ^ 1) for i in range(count)]
    jobs, done = list(jobs), []

    def beside(sent, pairs):
        got = exchange(sent, pairs)
        if jobs:
            result = jobs.pop(0)(done, lambda x: lax.optimization_barrier((sent, x))[1])
            got, first = lax.optimization_barrier((got, result[0]))
            done.append([first] + list(result[1:]))
        return got

    got = beside(sent, swap)
    total = done[0][0] + got.astype(F32)
    along_lon = [1 << k for k in range(1, lon.bit_length() - 1)]
    along_dp = [lon << k for k in range(dp.bit_length() - 1)]
    bits, other = along_lon + along_dp, along_dp + along_lon
    for even_bit, odd_bit in zip(bits, other):
        sent = total.astype(BF16)
        got = beside(
            sent, [(i, i ^ 1 ^ (odd_bit if i.bit_count() & 1 else even_bit)) for i in range(count)]
        )
        total = sent.astype(F32) + got.astype(F32)
    while jobs:
        done.append(jobs.pop(0)(done, lambda x: x))
    mine = (total * factor).astype(BF16)
    return mine, exchange(mine, swap), done


def per_device(fields, cotangent, kernel_first, kernel_second, metric):
    samples, c, n, lat = fields.shape
    counted = (
        float(samples * lax.axis_size("dp")) * float(n * lax.axis_size("lon")) * float(lat)
    )
    factor = jnp.float32(1.0 / counted**0.5)
    sent, jobs = one_sample(fields[0], cotangent[0], kernel_first, kernel_second, metric)
    mine, theirs, done = sum_everywhere(sent, jobs, factor)
    grad_first, grad_second = call(
        final_kernel, [((3, 3, c, c), BF16)] * 2, [], mine, theirs
    )
    return done[-1][0][None], grad_first, grad_second


def solution(mesh):
    placed = (P("dp", None, "lon", None), P("dp", None, "lon", None), P(), P(), P())
    return jax.shard_map(
        per_device,
        mesh=mesh,
        in_specs=placed,
        out_specs=(P("dp", None, "lon", None), P(), P()),
        check_vma=False,
    )
```
